512 devices in a mesh: tm: 128 (over y_hi, x, z), space: 4 (over y_lo, core).
Axes of the slice: x: 4, y: 8 (y_hi: 4, y_lo: 2; y = y_hi * 2 + y_lo), z: 8, core: 2. Of those that a mesh axis runs over, the one named last changes fastest.
Arguments:
- inputs: bfloat16 [128, 1, 144, 1280], P('tm', None, 'space'), may hold values from -120 to 120
- cotangent: bfloat16 [128, 1, 144, 1280], P('tm', None, 'space'), may hold values from -6 to 6
- norm_gain: bfloat16 [1280], replicated, may hold values from 0.5 to 1.5
- query_weight: bfloat16 [1280, 1280], P(None, 'space'), may hold values from -1.5 to 1.5
- key_weight: bfloat16 [1280, 1280], P(None, 'space'), may hold values from -1.5 to 1.5
- value_weight: bfloat16 [1280, 1280], P(None, 'space'), may hold values from -0.15625 to 0.15625
- output_weight: bfloat16 [1280, 1280], P('space'), may hold values from -0.15625 to 0.15625
Outputs:
- block_output: bfloat16 [128, 1, 144, 1280], P('tm', None, 'space')
- input_grads: bfloat16 [128, 1, 144, 1280], P('tm', None, 'space')
The draws below stay inside these ranges and needn't reach their ends.
All inputs are finite; a program needn't handle non-finite values.
Results may differ from the reference program's by a relative error of at most 0.018.
The reference program's roundings to bfloat16 on the way (of `hidden`, `probs_low`, `attended`, `out_grads`, `score_grads` and `query_grads`) count: a program that leaves them out, or rounds other values in their place, can miss the bound.
Values may be sent and summed in bfloat16 or wider, within the bound.
No kernel may reach another device: no remote copies, remote signals or barrier semaphores. Data moves between devices by JAX's collectives and lax.ppermute only.
A program may use at most 64 MiB of HBM per device.

```python
import jax
import jax.numpy as jnp
from jax import lax

C = 1280
HEADS = 20
HEAD_DIM = 64
POS = 144
CLIPS = 1
FRAMES = 128


def draw_inputs(key, part):
    key = jax.random.fold_in(key, 3)
    key_list = jax.random.split(key, 3)
    row_scale = jnp.exp(jax.random.uniform(key_list[0], (FRAMES, CLIPS, POS, 1), jnp.float32, 0.0, jnp.log(10.0)))
    chan_scale = jnp.exp(jax.random.uniform(key_list[1], (1, 1, 1, C), jnp.float32, jnp.log(0.3), jnp.log(3.0)))
    jitter = jax.random.truncated_normal(key_list[2], -4.0, 4.0, (FRAMES, CLIPS, POS, C), jnp.float32)
    result = jitter * chan_scale * row_scale
    return jnp.clip(result, -120.0, 120.0).astype(jnp.bfloat16)


def draw_query_weight(key, part):
    private_key = jax.random.fold_in(key, 1)
    private = jax.random.normal(private_key, (C, C), jnp.float32) * C ** (-0.5)
    result = private
    return jnp.clip(result, -1.5, 1.5).astype(jnp.bfloat16)


def draw_key_weight(key, part):
    private_key = jax.random.fold_in(key, 2)
    private = jax.random.normal(private_key, (C, C), jnp.float32) * C ** (-0.5)
    result = private
    return jnp.clip(result, -1.5, 1.5).astype(jnp.bfloat16)


def shard_levels(rng, dims, cuts, least, largest):
    def one(dim, shards_of):
        steps = jax.random.uniform(jax.random.fold_in(jax.random.fold_in(rng, 6), dim), (shards_of,), jnp.float32, least / len(cuts), largest / len(cuts))
        return jnp.repeat(jnp.exp(steps), dims[dim] // shards_of).reshape((-1,) + (1,) * (len(dims) - dim - 1))

    level = one(*cuts[0])
    for cut in cuts[1:]:
        level = level * one(*cut)
    return level


def bell_draw(stream_key, shape, scale, reach, shards=(), kind=jnp.bfloat16):
    loudness = shard_levels(stream_key, shape, shards, -0.22, 0.18) if shards else 1.0
    entries = jax.random.normal(stream_key, shape, jnp.float32) * scale * loudness
    return jnp.minimum(jnp.maximum(entries, -reach), reach).astype(kind)


def setup_inputs(seed: int = 0) -> dict:
    key_of = jax.random.split(jax.random.key(seed), 8)
    inputs = draw_inputs(jax.random.fold_in(key_of[7], 71), 0)
    cotangent = bell_draw(key_of[1], (FRAMES, CLIPS, POS, C), 1.0, 6.0, ((0, 128), (2, 4)))
    norm_gain = jnp.clip(1.0 + 0.1 * jax.random.normal(key_of[2], (C,), jnp.float32), 0.5, 1.5).astype(jnp.bfloat16)
    query_weight = draw_query_weight(jax.random.fold_in(key_of[7], 71), 0)
    key_weight = draw_key_weight(jax.random.fold_in(key_of[7], 71), 0)
    value_weight = bell_draw(key_of[5], (C, C), C ** -0.5, 0.15625, ((1, 4),))
    output_weight = bell_draw(key_of[6], (C, C), C ** -0.5, 0.15625, ((0, 4),))
    return {"inputs": inputs, "cotangent": cotangent, "norm_gain": norm_gain, "query_weight": query_weight, "key_weight": key_weight, "value_weight": value_weight, "output_weight": output_weight}


EPSILON = 1e-05
NEG_FILL = -1e+30
OFFSETS = (-2, -1, 0, 1, 2)

def moved(tensor, offset):
    if offset == 0:
        return tensor
    filler = jnp.zeros((abs(offset),) + tensor.shape[1:], tensor.dtype)
    if offset > 0:
        return jnp.concatenate([tensor[offset:], filler], axis=0)
    return jnp.concatenate([filler, tensor[:offset]], axis=0)

def rounded(tensor):
    return lax.optimization_barrier(tensor.astype(jnp.bfloat16)).astype(jnp.float32)

def reference(inputs, cotangent, norm_gain, query_weight, key_weight, value_weight, output_weight):
    score_scale = HEAD_DIM ** (-0.5)
    gain_values = norm_gain.astype(jnp.float32)
    values = inputs.astype(jnp.float32)
    center = lax.optimization_barrier(jnp.mean(values, axis=-1, keepdims=True))
    spread = lax.optimization_barrier(jnp.mean(jnp.square(values - center), axis=-1, keepdims=True))
    inverse = lax.rsqrt(spread + EPSILON)
    normed = (values - center) * inverse
    hidden = (normed * gain_values).astype(jnp.bfloat16).reshape(-1, C)
    head_shape = (FRAMES, CLIPS, POS, HEADS, HEAD_DIM)

    def project(weight):
        return jnp.dot(hidden, weight, preferred_element_type=jnp.float32).astype(jnp.bfloat16).reshape(head_shape)
    queries = project(query_weight)
    keys_all = project(key_weight)
    vals_all = project(value_weight)
    query_f = queries.astype(jnp.float32)
    frame_ids = jnp.arange(FRAMES, dtype=jnp.int32)
    score_list = []
    range_list = []
    for offset in OFFSETS:
        score_list.append(lax.optimization_barrier(jnp.sum(query_f * moved(keys_all, offset).astype(jnp.float32), axis=-1)) * score_scale)
        range_list.append(((frame_ids + offset >= 0) & (frame_ids + offset < FRAMES))[:, None, None, None])
    scores = jnp.stack(score_list)
    in_range = jnp.stack(range_list)
    masked = jnp.where(in_range, scores, NEG_FILL)
    row_max = lax.optimization_barrier(jnp.max(masked, axis=0))
    exponent = jnp.exp(masked - row_max)
    attention = exponent / lax.optimization_barrier(jnp.sum(exponent, axis=0))
    probs_low = rounded(attention)
    attended = jnp.zeros(head_shape, jnp.float32)
    for position, offset in enumerate(OFFSETS):
        attended = attended + probs_low[position][..., None] * moved(vals_all, offset).astype(jnp.float32)
    attended = attended.astype(jnp.bfloat16).reshape(-1, C)
    projected = jnp.dot(attended, output_weight, preferred_element_type=jnp.float32).reshape(values.shape)
    block_output = (values + projected).astype(jnp.bfloat16)
    out_grads = jnp.dot(cotangent.reshape(-1, C), output_weight.T, preferred_element_type=jnp.float32)
    grads_f = rounded(out_grads).reshape(head_shape)
    prob_grads = jnp.stack([lax.optimization_barrier(jnp.sum(grads_f * moved(vals_all, offset).astype(jnp.float32), axis=-1)) for offset in OFFSETS])
    row_delta = lax.optimization_barrier(jnp.sum(attention * prob_grads, axis=0))
    score_grads = rounded(attention * (prob_grads - row_delta))
    query_grads = jnp.zeros(head_shape, jnp.float32)
    key_grads = jnp.zeros(head_shape, jnp.float32)
    value_grads = jnp.zeros(head_shape, jnp.float32)
    for position, offset in enumerate(OFFSETS):
        query_grads = query_grads + score_grads[position][..., None] * moved(keys_all, offset).astype(jnp.float32)
        key_grads = key_grads + moved(score_grads[position][..., None] * query_f, -offset)
        value_grads = value_grads + moved(probs_low[position][..., None] * grads_f, -offset)
    query_low = (query_grads * score_scale).astype(jnp.bfloat16).reshape(-1, C)
    key_low = (key_grads * score_scale).astype(jnp.bfloat16).reshape(-1, C)
    value_low = value_grads.astype(jnp.bfloat16).reshape(-1, C)
    hidden_grads = jnp.dot(query_low, query_weight.T, preferred_element_type=jnp.float32)
    hidden_grads = hidden_grads + jnp.dot(key_low, key_weight.T, preferred_element_type=jnp.float32)
    hidden_grads = hidden_grads + jnp.dot(value_low, value_weight.T, preferred_element_type=jnp.float32)
    scaled = hidden_grads.reshape(values.shape) * gain_values
    layer_grads = inverse * (scaled - lax.optimization_barrier(jnp.mean(scaled, axis=-1, keepdims=True)) - normed * lax.optimization_barrier(jnp.mean(scaled * normed, axis=-1, keepdims=True)))
    input_grads = (cotangent.astype(jnp.float32) + layer_grads).astype(jnp.bfloat16)
    return (block_output, input_grads)
```

```python
import functools

import jax
import jax.numpy as jnp
from jax import lax
from jax.experimental import pallas as pl
from jax.experimental.pallas import tpu as pltpu
from jax.sharding import PartitionSpec as P

HEAD_DIM = 64
EPSILON = 1e-05
NEG_FILL = -1e30
ORDERED = (-2, -1, 0, 1, 2)
OFFSETS = (-2, -1, 1, 2)
SHARDS = 4
BF16 = jnp.bfloat16
F32 = jnp.float32

VMEM = pl.BlockSpec(memory_space=pltpu.VMEM)
SMEM = pl.BlockSpec(memory_space=pltpu.SMEM)
PARAMS = pltpu.CompilerParams(vmem_limit_bytes=48 * 1024 * 1024)


def dot(a, b):
    return lax.dot_general(a, b, (((1,), (0,)), ((), ())), preferred_element_type=F32)


def dot_t(a, b):
    return lax.dot_general(a, b, (((1,), (1,)), ((), ())), preferred_element_type=F32)


def normalized(x):
    center = jnp.mean(x, axis=-1, keepdims=True)
    shifted = x - center
    spread = jnp.mean(jnp.square(shifted), axis=-1, keepdims=True)
    inverse = lax.rsqrt(spread + EPSILON)
    return shifted * inverse, inverse


def norm_kernel(x_ref, cot_ref, gain_ref, out_ref):
    normed, _ = normalized(x_ref[...].astype(F32))
    out_ref[0] = (normed * gain_ref[...].astype(F32)).astype(BF16)
    out_ref[1] = cot_ref[...]


def project_kernel(g_ref, wq_ref, wk_ref, wv_ref, wo_ref, a_ref, b_ref, rows_ref):
    piece = g_ref.shape[2]

    def gathered(which):
        for s in range(SHARDS):
            rows_ref[piece * s : piece * (s + 1), :] = g_ref[s, which].astype(F32)
        return rows_ref[...].astype(BF16)

    hidden = gathered(0)
    keys = dot_t(hidden, wk_ref[...])
    vals = dot_t(hidden, wv_ref[...])
    b_ref[...] = jnp.concatenate([keys, vals], axis=1).astype(BF16)
    queries = dot_t(hidden, wq_ref[...])
    out_grads = dot_t(gathered(1), wo_ref[...])
    a_ref[...] = jnp.concatenate([queries, out_grads], axis=1).astype(BF16)


def head_lanes(width):
    lane = lax.broadcasted_iota(jnp.int32, (width, 256), 0) // HEAD_DIM
    col = lax.broadcasted_iota(jnp.int32, (width, 256), 1)
    heads = width // HEAD_DIM // 2
    want = jnp.where(lane < heads, lane, lane - heads + 128)
    return (col == want).astype(BF16)


def attend_kernel(frames, frame_ref, a_ref, *refs):
    b_refs = refs[:5]
    send_refs, own_ref, mixed_ref = refs[5:9], refs[9], refs[10]
    frame = frame_ref[0]
    a = a_ref[...].astype(F32)
    width = a.shape[1]
    reduce_mat = head_lanes(width)
    scores, prob_grads = [], []
    for offset, b_ref in zip(ORDERED, b_refs):
        product = a * b_ref[...].astype(F32)
        high = product.astype(BF16)
        low = (product - high.astype(F32)).astype(BF16)
        sums = dot(high, reduce_mat) + dot(low, reduce_mat)
        present = (frame + offset >= 0) & (frame + offset < frames)
        scores.append(jnp.where(present, sums[:, :128] * (HEAD_DIM**-0.5), NEG_FILL))
        prob_grads.append(sums[:, 128:])
    row_max = functools.reduce(jnp.maximum, scores)
    exponent = [jnp.exp(s - row_max) for s in scores]
    denominator = sum(exponent)
    attention = [e / denominator for e in exponent]
    row_delta = sum(p * g for p, g in zip(attention, prob_grads))
    mixed = jnp.zeros_like(a)
    scale = jnp.where(
        lax.broadcasted_iota(jnp.int32, a.shape, 1) < width // 2, HEAD_DIM**-0.5, 1.0
    )
    scaled_a = a * scale
    sends = iter(send_refs)
    for offset, b_ref, p, g in zip(ORDERED, b_refs, attention, prob_grads):
        score_grads = (p * (g - row_delta)).astype(BF16)
        small = jnp.concatenate([score_grads, p.astype(BF16)], axis=1)
        weights = dot_t(small, reduce_mat)
        mixed = mixed + weights * b_ref[...].astype(F32)
        if offset == 0:
            own_ref[...] = weights * scaled_a
        else:
            next(sends)[...] = (weights * scaled_a).astype(BF16)
    mixed_ref[...] = (mixed * scale).astype(BF16)


def output_kernel(mixed_ref, wo_ref, out_ref, rows_ref):
    half = mixed_ref.shape[1] // 2
    piece = out_ref.shape[1]
    rows_ref[...] = dot(mixed_ref[:, half:], wo_ref[...])
    for s in range(SHARDS):
        out_ref[s] = rows_ref[piece * s : piece * (s + 1), :].astype(BF16)


def hidden_kernel(mixed_ref, own_ref, r0, r1, r2, r3, wq_ref, wk_ref, wv_ref, out_ref, rows_ref):
    half = mixed_ref.shape[1] // 2
    piece = out_ref.shape[1]
    total = own_ref[...]
    for r in (r0, r1, r2, r3):
        total = total + r[...].astype(F32)
    total = total.astype(BF16)
    rows_ref[...] = (
        dot(mixed_ref[:, :half], wq_ref[...])
        + dot(total[:, :half], wk_ref[...])
        + dot(total[:, half:], wv_ref[...])
    )
    for s in range(SHARDS):
        out_ref[s] = rows_ref[piece * s : piece * (s + 1), :].astype(BF16)


def finish_kernel(x_ref, cot_ref, gain_ref, out_parts, grad_parts, block_ref, grads_ref):
    x = x_ref[...].astype(F32)
    block_ref[...] = (x + sum(out_parts[s].astype(F32) for s in range(SHARDS))).astype(BF16)
    normed, inverse = normalized(x)
    scaled = sum(grad_parts[s].astype(F32) for s in range(SHARDS)) * gain_ref[...].astype(F32)
    layer_grads = inverse * (
        scaled
        - jnp.mean(scaled, axis=-1, keepdims=True)
        - normed * jnp.mean(scaled * normed, axis=-1, keepdims=True)
    )
    grads_ref[...] = (cot_ref[...].astype(F32) + layer_grads).astype(BF16)


def call(kernel, out_shape, in_specs, scratch=(), flops=0, bytes_accessed=0):
    return pl.pallas_call(
        kernel,
        out_shape=out_shape,
        in_specs=in_specs,
        out_specs=jax.tree.map(lambda _: VMEM, out_shape),
        scratch_shapes=list(scratch),
        compiler_params=PARAMS,
        cost_estimate=pl.CostEstimate(flops=flops, bytes_accessed=bytes_accessed, transcendentals=0),
    )


def passed_along(block, distance):
    count = lax.axis_size("tm")
    route = [(i, i + distance) for i in range(count) if 0 <= i + distance < count]
    return lax.ppermute(block, "tm", route)


def swapped(parts):
    return lax.all_to_all(parts, "space", 0, 0)


def per_device(inputs, cotangent, norm_gain, query_weight, key_weight, value_weight, output_weight):
    frame = lax.axis_index("tm").astype(jnp.int32).reshape(1)
    frames = lax.axis_size("tm")
    piece, channels = inputs.shape[2:]
    rows, local = piece * SHARDS, query_weight.shape[1]
    x = inputs.reshape(piece, channels)
    cot = cotangent.reshape(piece, channels)
    gain = norm_gain.reshape(1, channels)
    wq, wk, wv = query_weight.T, key_weight.T, value_weight.T
    wo = output_weight
    shape = jax.ShapeDtypeStruct

    both = call(norm_kernel, shape((2, piece, channels), BF16), [VMEM] * 3)(x, cot, gain)
    gathered = lax.all_gather(both, "space", axis=0)
    a, b = call(
        project_kernel,
        (shape((rows, 2 * local), BF16), shape((rows, 2 * local), BF16)),
        [VMEM] * 5,
        [pltpu.VMEM((rows, channels), F32)],
    )(gathered, wq, wk, wv, wo)
    near = {offset: passed_along(b, -offset) for offset in OFFSETS}
    near[0] = b
    wide = shape((rows, 2 * local), BF16)
    *sends, own, mixed = call(
        functools.partial(attend_kernel, frames),
        (wide, wide, wide, wide, shape((rows, 2 * local), F32), wide),
        [SMEM] + [VMEM] * 6,
    )(frame, a, *[near[offset] for offset in ORDERED])
    arrived = [passed_along(send, offset) for offset, send in zip(OFFSETS, sends)]
    parts = shape((SHARDS, piece, channels), BF16)
    out_parts = call(output_kernel, parts, [VMEM] * 2, [pltpu.VMEM((rows, channels), F32)])(mixed, wo)
    out_parts = swapped(out_parts)
    grad_parts = call(hidden_kernel, parts, [VMEM] * 9, [pltpu.VMEM((rows, channels), F32)])(
        mixed, own, *arrived, wq, wk, wv
    )
    grad_parts = swapped(grad_parts)
    block, grads = call(
        finish_kernel, (shape((piece, channels), BF16), shape((piece, channels), BF16)), [VMEM] * 5
    )(x, cot, gain, out_parts, grad_parts)
    return block.reshape(inputs.shape), grads.reshape(inputs.shape)


def solution(mesh):
    placed = (
        P("tm", None, "space", None),
        P("tm", None, "space", None),
        P(),
        P(None, "space"),
        P(None, "space"),
        P(None, "space"),
        P("space", None),
    )
    return jax.shard_map(
        per_device,
        mesh=mesh,
        in_specs=placed,
        out_specs=(P("tm", None, "space", None), P("tm", None, "space", None)),
        check_vma=False,
    )
```

```python
import functools

import jax
import jax.numpy as jnp
from jax import lax
from jax.experimental import pallas as pl
from jax.experimental.pallas import tpu as pltpu
from jax.sharding import Mesh
from jax.sharding import PartitionSpec as P

HEAD_DIM = 64
EPSILON = 1e-05
NEG_FILL = -1e30
ORDERED = (-2, -1, 0, 1, 2)
PAIR = 2
SHARDS = 4
BF16 = jnp.bfloat16
F32 = jnp.float32

VMEM = pl.BlockSpec(memory_space=pltpu.VMEM)
SMEM = pl.BlockSpec(memory_space=pltpu.SMEM)
PARAMS = pltpu.CompilerParams(vmem_limit_bytes=12 * 1024 * 1024)


def dot(a, b):
    return lax.dot_general(a, b, (((1,), (0,)), ((), ())), preferred_element_type=F32)


def dot_t(a, b):
    return lax.dot_general(a, b, (((1,), (1,)), ((), ())), preferred_element_type=F32)


def normalized(x):
    center = jnp.mean(x, axis=-1, keepdims=True)
    shifted = x - center
    spread = jnp.mean(jnp.square(shifted), axis=-1, keepdims=True)
    inverse = lax.rsqrt(spread + EPSILON)
    return shifted * inverse, inverse


def norm_kernel(x_ref, cot_ref, gain_ref, out_ref):
    half = x_ref.shape[0] // PAIR
    normed, _ = normalized(x_ref[...].astype(F32))
    hidden = normed * gain_ref[...].astype(F32)
    cot = cot_ref[...].astype(F32)
    for h in range(PAIR):
        rows = slice(h * half, (h + 1) * half)
        out_ref[h] = jnp.concatenate([hidden[rows], cot[rows]], axis=0).astype(BF16)


def gathered(g_ref, rows_ref, which):
    half = g_ref.shape[2] // 2
    for frame in range(PAIR):
        for s in range(SHARDS):
            start = (frame * SHARDS + s) * half
            rows_ref[start : start + half, :] = g_ref[
                s, frame, which * half : (which + 1) * half
            ].astype(F32)
    return rows_ref[...].astype(BF16)


def key_value_kernel(g_ref, wk_ref, wv_ref, b_ref, rows_ref):
    hidden = gathered(g_ref, rows_ref, 0)
    keys = dot_t(hidden, wk_ref[...])
    vals = dot_t(hidden, wv_ref[...])
    b_ref[...] = jnp.concatenate([keys, vals], axis=1).astype(BF16)


def query_kernel(g_ref, wq_ref, wo_ref, a_ref, rows_ref):
    queries = dot_t(gathered(g_ref, rows_ref, 0), wq_ref[...])
    out_grads = dot_t(gathered(g_ref, rows_ref, 1), wo_ref[...])
    a_ref[...] = jnp.concatenate([queries, out_grads], axis=1).astype(BF16)


def head_lanes(width):
    lane = lax.broadcasted_iota(jnp.int32, (width, 256), 0) // HEAD_DIM
    col = lax.broadcasted_iota(jnp.int32, (width, 256), 1)
    heads = width // HEAD_DIM // 2
    want = jnp.where(lane < heads, lane, lane - heads + 128)
    return (col == want).astype(BF16)


def attend_kernel(
    frames, pair_ref, a_ref, b_ref, even_ref, odd_ref, even_out, odd_out, own_ref, mixed_ref, near_ref, grads_ref
):
    pair = pair_ref[0]
    is_even = pair % 2 == 0
    rows, width = a_ref.shape
    one = rows // PAIR
    from_even = even_ref[...].astype(F32)
    from_odd = odd_ref[...].astype(F32)
    near_ref[0:rows] = jnp.where(is_even, from_odd, from_even)
    near_ref[rows : 2 * rows] = b_ref[...].astype(F32)
    near_ref[2 * rows : 3 * rows] = jnp.where(is_even, from_even, from_odd)
    a = a_ref[...].astype(F32)
    reduce_mat = head_lanes(width)
    frame = pair * PAIR + lax.broadcasted_iota(jnp.int32, (rows, 128), 0) // one
    scores, prob_grads = [], []
    for offset in ORDERED:
        start = (offset + 2) * one
        product = a * near_ref[start : start + rows]
        high = product.astype(BF16)
        low = (product - high.astype(F32)).astype(BF16)
        sums = dot(high, reduce_mat) + dot(low, reduce_mat)
        present = (frame + offset >= 0) & (frame + offset < frames)
        scores.append(jnp.where(present, sums[:, :128] * (HEAD_DIM**-0.5), NEG_FILL))
        prob_grads.append(sums[:, 128:])
    row_max = functools.reduce(jnp.maximum, scores)
    exponent = [jnp.exp(s - row_max) for s in scores]
    denominator = sum(exponent)
    attention = [e / denominator for e in exponent]
    row_delta = sum(p * g for p, g in zip(attention, prob_grads))
    mixed = jnp.zeros_like(a)
    scale = jnp.where(lax.broadcasted_iota(jnp.int32, a.shape, 1) < width // 2, HEAD_DIM**-0.5, 1.0)
    scaled_a = a * scale
    grads_ref[...] = jnp.zeros_like(grads_ref)
    for offset, p, g in zip(ORDERED, attention, prob_grads):
        start = (offset + 2) * one
        score_grads = (p * (g - row_delta)).astype(BF16)
        small = jnp.concatenate([score_grads, p.astype(BF16)], axis=1)
        weights = dot_t(small, reduce_mat)
        mixed = mixed + weights * near_ref[start : start + rows]
        grads_ref[start : start + rows] += weights * scaled_a
    mixed_ref[...] = (mixed * scale).astype(BF16)
    before = grads_ref[0:rows]
    after = grads_ref[2 * rows : 3 * rows]
    even_out[...] = jnp.where(is_even, after, before).astype(BF16)
    odd_out[...] = jnp.where(is_even, before, after).astype(BF16)
    own_ref[...] = grads_ref[rows : 2 * rows]


def back_kernel(mixed_ref, own_ref, even_ref, odd_ref, wq_ref, wk_ref, wv_ref, wo_ref, parts_ref, rows_ref):
    width = mixed_ref.shape[1] // 2
    half = parts_ref.shape[1] // 2
    total = own_ref[...] + even_ref[...].astype(F32) + odd_ref[...].astype(F32)
    total = total.astype(BF16)
    rows_ref[0] = dot(mixed_ref[:, width:], wo_ref[...])
    rows_ref[1] = (
        dot(mixed_ref[:, :width], wq_ref[...])
        + dot(total[:, :width], wk_ref[...])
        + dot(total[:, width:], wv_ref[...])
    )
    for part in range(PAIR * SHARDS):
        rows = slice(part * half, (part + 1) * half)
        parts_ref[part] = jnp.concatenate([rows_ref[0, rows], rows_ref[1, rows]], axis=0).astype(BF16)


def finish_kernel(x_ref, cot_ref, gain_ref, parts_ref, block_ref, grads_ref):
    half = parts_ref.shape[1] // 2
    summed = [
        sum(parts_ref[h * SHARDS + s].astype(F32) for s in range(SHARDS)) for h in range(PAIR)
    ]
    out = jnp.concatenate([part[:half] for part in summed], axis=0)
    hidden_grads = jnp.concatenate([part[half:] for part in summed], axis=0)
    x = x_ref[...].astype(F32)
    block_ref[...] = (x + out).astype(BF16)
    normed, inverse = normalized(x)
    scaled = hidden_grads * gain_ref[...].astype(F32)
    layer_grads = inverse * (
        scaled
        - jnp.mean(scaled, axis=-1, keepdims=True)
        - normed * jnp.mean(scaled * normed, axis=-1, keepdims=True)
    )
    grads_ref[...] = (cot_ref[...].astype(F32) + layer_grads).astype(BF16)


def call(kernel, out_shape, in_specs, scratch=(), flops=0, bytes_accessed=0):
    return pl.pallas_call(
        kernel,
        out_shape=out_shape,
        in_specs=in_specs,
        out_specs=jax.tree.map(lambda _: VMEM, out_shape),
        scratch_shapes=list(scratch),
        compiler_params=PARAMS,
        cost_estimate=pl.CostEstimate(flops=flops, bytes_accessed=bytes_accessed, transcendentals=0),
    )


def exchanged(block, first):
    count = lax.axis_size("pair")
    route = []
    for i in range(first, count - 1, 2):
        route += [(i, i + 1), (i + 1, i)]
    return lax.ppermute(block, "pair", route)


def per_device(inputs, cotangent, norm_gain, query_weight, key_weight, value_weight, output_weight):
    pair = lax.axis_index("pair").astype(jnp.int32).reshape(1)
    frames = lax.axis_size("pair") * PAIR
    piece, channels = inputs.shape[2:]
    rows, local = piece * SHARDS, query_weight.shape[1]
    x = inputs.reshape(piece, channels)
    cot = cotangent.reshape(piece, channels)
    gain = norm_gain.reshape(1, channels)
    wq, wk, wv, wo = query_weight.T, key_weight.T, value_weight.T, output_weight
    shape = jax.ShapeDtypeStruct
    wide = shape((rows, 2 * local), BF16)
    row_scratch = pltpu.VMEM((rows, channels), F32)
    near_scratch = pltpu.VMEM((3 * rows, 2 * local), F32)

    halves = call(norm_kernel, shape((PAIR, piece, channels), BF16), [VMEM] * 3)(x, cot, gain)
    halves = lax.all_to_all(halves, "half", 0, 0)
    every = lax.all_gather(halves, "space", axis=0)
    b = call(key_value_kernel, wide, [VMEM] * 3, [row_scratch])(every, wk, wv)
    near = [exchanged(b, first) for first in (0, 1)]
    a = call(query_kernel, wide, [VMEM] * 3, [row_scratch])(every, wq, wo)
    *sends, own, mixed = call(
        functools.partial(attend_kernel, frames),
        (wide, wide, shape((rows, 2 * local), F32), wide),
        [SMEM] + [VMEM] * 4,
        [near_scratch, near_scratch],
    )(pair, a, b, *near)
    arrived = [exchanged(send, first) for first, send in zip((0, 1), sends)]
    parts = call(
        back_kernel,
        shape((PAIR * SHARDS, piece, channels), BF16),
        [VMEM] * 8,
        [pltpu.VMEM((2, rows, channels), F32)],
    )(mixed, own, *arrived, wq, wk, wv, wo)
    parts = lax.all_to_all(parts, ("half", "space"), 0, 0)
    block, grads = call(
        finish_kernel, (shape((piece, channels), BF16), shape((piece, channels), BF16)), [VMEM] * 4
    )(x, cot, gain, parts)
    return block.reshape(inputs.shape), grads.reshape(inputs.shape)


def solution(mesh):
    devices = mesh.devices.reshape(-1, PAIR, SHARDS)
    mesh = Mesh(devices, ("pair", "half", "space"))
    frames = ("pair", "half")
    placed = (
        P(frames, None, "space", None),
        P(frames, None, "space", None),
        P(),
        P(None, "space"),
        P(None, "space"),
        P(None, "space"),
        P("space", None),
    )
    return jax.shard_map(
        per_device,
        mesh=mesh,
        in_specs=placed,
        out_specs=(P(frames, None, "space", None), P(frames, None, "space", None)),
        check_vma=False,
    )
```

```python
import functools

import jax
import jax.numpy as jnp
from jax import lax
from jax.experimental import pallas as pl
from jax.experimental.pallas import tpu as pltpu
from jax.sharding import Mesh
from jax.sharding import PartitionSpec as P

HEAD_DIM = 64
HEAD_SHIFT = 6
EPSILON = 1e-05
NEG_FILL = -1e30
ORDERED = (-2, -1, 0, 1, 2)
PAIR = 2
SHARDS = 4
BF16 = jnp.bfloat16
F32 = jnp.float32

VMEM = pl.BlockSpec(memory_space=pltpu.VMEM)
SMEM = pl.BlockSpec(memory_space=pltpu.SMEM)
PARAMS = pltpu.CompilerParams(vmem_limit_bytes=12 * 1024 * 1024)


def dot(a, b):
    return lax.dot_general(a, b, (((1,), (0,)), ((), ())), preferred_element_type=F32)


def dot_t(a, b):
    return lax.dot_general(a, b, (((1,), (1,)), ((), ())), preferred_element_type=F32)


def normalized(x):
    center = jnp.mean(x, axis=-1, keepdims=True)
    shifted = x - center
    spread = jnp.mean(jnp.square(shifted), axis=-1, keepdims=True)
    inverse = lax.rsqrt(spread + EPSILON)
    return shifted * inverse, inverse


def norm_kernel(x_hbm, cot_hbm, gain_hbm, out_ref, x_ref, cot_ref, gain_ref, sems):
    copies = [
        pltpu.make_async_copy(source, target, sems.at[i])
        for i, (source, target) in enumerate(
            ((x_hbm, x_ref), (gain_hbm, gain_ref), (cot_hbm, cot_ref))
        )
    ]
    for copy in copies:
        copy.start()
    half = x_ref.shape[0] // PAIR
    copies[0].wait()
    normed, _ = normalized(x_ref[...].astype(F32))
    copies[1].wait()
    hidden = normed * gain_ref[...].astype(F32).reshape(1, -1)
    copies[2].wait()
    cot = cot_ref[...].astype(F32)
    for h in range(PAIR):
        rows = slice(h * half, (h + 1) * half)
        out_ref[h] = jnp.concatenate([hidden[rows], cot[rows]], axis=0).astype(BF16)


def take_kernel(halves_ref, hidden_ref, cot_ref):
    half = halves_ref.shape[1] // 2
    both = [halves_ref[f].astype(F32) for f in range(PAIR)]
    hidden_ref[...] = jnp.concatenate([v[:half] for v in both], axis=0).astype(BF16)
    cot_ref[...] = jnp.concatenate([v[half:] for v in both], axis=0).astype(BF16)


def gathered(g_ref, rows_ref):
    half = g_ref.shape[1] // PAIR
    for frame in range(PAIR):
        for s in range(SHARDS):
            start = (frame * SHARDS + s) * half
            rows_ref[start : start + half, :] = g_ref[s, frame * half : (frame + 1) * half].astype(F32)
    return rows_ref[...].astype(BF16)


def key_value_kernel(g_ref, wk_ref, wv_ref, b_ref, rows_ref):
    hidden = gathered(g_ref, rows_ref)
    keys = dot_t(hidden, wk_ref[...])
    vals = dot_t(hidden, wv_ref[...])
    b_ref[...] = jnp.concatenate([keys, vals], axis=1).astype(BF16)


def query_kernel(hidden_ref, cot_ref, wq_ref, wo_ref, a_ref, rows_ref):
    queries = dot_t(gathered(hidden_ref, rows_ref), wq_ref[...])
    out_grads = dot_t(gathered(cot_ref, rows_ref), wo_ref[...])
    a_ref[...] = jnp.concatenate([queries, out_grads], axis=1).astype(BF16)


def head_lanes(width, transposed=False):
    shape = (256, width) if transposed else (width, 256)
    lane = lax.broadcasted_iota(jnp.int32, shape, 1 if transposed else 0) >> HEAD_SHIFT
    col = lax.broadcasted_iota(jnp.int32, shape, 0 if transposed else 1)
    heads = (width >> HEAD_SHIFT) // 2
    want = jnp.where(lane < heads, lane, lane - heads + 128)
    return (col == want).astype(BF16)


def build_near(pair_ref, b_ref, even_ref, odd_ref, near_ref):
    rows = b_ref.shape[0]
    is_even = pair_ref[0] % 2 == 0
    from_even = even_ref[...].astype(F32)
    from_odd = odd_ref[...].astype(F32)
    near_ref[0:rows] = jnp.where(is_even, from_odd, from_even)
    near_ref[rows : 2 * rows] = b_ref[...].astype(F32)
    near_ref[2 * rows : 3 * rows] = jnp.where(is_even, from_even, from_odd)


def lane_scale(shape):
    lane = lax.broadcasted_iota(jnp.int32, shape, 1)
    return jnp.where(lane < shape[1] // 2, HEAD_DIM**-0.5, 1.0)


def attend_kernel(
    frames, pair_ref, a_ref, b_ref, even_ref, odd_ref, even_out, odd_out, own_ref, small_ref, near_ref
):
    pair = pair_ref[0]
    rows, width = a_ref.shape
    one = rows // PAIR
    build_near(pair_ref, b_ref, even_ref, odd_ref, near_ref)
    a = a_ref[...].astype(F32)
    reduce_mat = head_lanes(width)
    later = lax.broadcasted_iota(jnp.int32, (rows, 128), 0) >= one
    frame = pair * PAIR + later.astype(jnp.int32)
    scores, prob_grads = [], []
    for offset in ORDERED:
        start = (offset + 2) * one
        product = a * near_ref[start : start + rows]
        high = product.astype(BF16)
        low = (product - high.astype(F32)).astype(BF16)
        sums = dot(high, reduce_mat) + dot(low, reduce_mat)
        present = (frame + offset >= 0) & (frame + offset < frames)
        scores.append(jnp.where(present, sums[:, :128] * (HEAD_DIM**-0.5), NEG_FILL))
        prob_grads.append(sums[:, 128:])
    row_max = functools.reduce(jnp.maximum, scores)
    exponent = [jnp.exp(s - row_max) for s in scores]
    denominator = sum(exponent)
    attention = [e / denominator for e in exponent]
    row_delta = sum(p * g for p, g in zip(attention, prob_grads))
    scaled_a = a * lane_scale(a.shape)
    spread_mat = head_lanes(width, transposed=True)
    sent = []
    for i, (p, g) in enumerate(zip(attention, prob_grads)):
        score_grads = (p * (g - row_delta)).astype(BF16)
        small = jnp.concatenate([score_grads, p.astype(BF16)], axis=1)
        small_ref[i] = small
        sent.append(dot(small, spread_mat) * scaled_a)
    segments = []
    for i in range(len(ORDERED) + 1):
        terms = []
        if i < len(ORDERED):
            terms.append(sent[i][:one])
        if i > 0:
            terms.append(sent[i - 1][one:])
        segments.append(sum(terms))
    before = jnp.concatenate(segments[0:2], axis=0)
    after = jnp.concatenate(segments[4:6], axis=0)
    is_even = pair % 2 == 0
    even_out[...] = jnp.where(is_even, after, before).astype(BF16)
    odd_out[...] = jnp.where(is_even, before, after).astype(BF16)
    own_ref[0:one] = segments[2]
    own_ref[one:rows] = segments[3]


def mix_kernel(
    pair_ref, small_ref, b_ref, even_ref, odd_ref, wq_ref, wo_ref, out_ref, query_part_ref, near_ref
):
    build_near(pair_ref, b_ref, even_ref, odd_ref, near_ref)
    rows, width = b_ref.shape
    one, half = rows // PAIR, width // 2
    reduce_mat = head_lanes(width)
    mixed = jnp.zeros((rows, width), F32)
    for i in range(len(ORDERED)):
        mixed = mixed + dot_t(small_ref[i], reduce_mat) * near_ref[i * one : i * one + rows]
    mixed = (mixed * lane_scale(mixed.shape)).astype(BF16)
    query_part_ref[...] = dot(mixed[:, :half], wq_ref[...])
    out_ref[...] = dot(mixed[:, half:], wo_ref[...])


def back_kernel(out_ref, query_part_ref, own_ref, even_ref, odd_ref, wk_ref, wv_ref, parts_ref, rows_ref):
    width = own_ref.shape[1] // 2
    half = parts_ref.shape[1] // 2
    total = own_ref[...] + even_ref[...].astype(F32) + odd_ref[...].astype(F32)
    total = total.astype(BF16)
    rows_ref[...] = (
        query_part_ref[...]
        + dot(total[:, :width], wk_ref[...])
        + dot(total[:, width:], wv_ref[...])
    )
    for part in range(PAIR * SHARDS):
        rows = slice(part * half, (part + 1) * half)
        parts_ref[part] = jnp.concatenate([out_ref[rows], rows_ref[rows]], axis=0).astype(BF16)


def finish_kernel(x_ref, cot_ref, gain_ref, parts_ref, block_ref, grads_ref):
    half = parts_ref.shape[1] // 2
    summed = [
        sum(parts_ref[h * SHARDS + s].astype(F32) for s in range(SHARDS)) for h in range(PAIR)
    ]
    out = jnp.concatenate([part[:half] for part in summed], axis=0)
    hidden_grads = jnp.concatenate([part[half:] for part in summed], axis=0)
    x = x_ref[...].astype(F32)
    block_ref[...] = (x + out).astype(BF16)
    normed, inverse = normalized(x)
    scaled = hidden_grads * gain_ref[...].astype(F32).reshape(1, -1)
    layer_grads = inverse * (
        scaled
        - jnp.mean(scaled, axis=-1, keepdims=True)
        - normed * jnp.mean(scaled * normed, axis=-1, keepdims=True)
    )
    grads_ref[...] = (cot_ref[...].astype(F32) + layer_grads).astype(BF16)


def call(kernel, out_shape, in_specs, scratch=(), flops=0, bytes_accessed=0):
    return pl.pallas_call(
        kernel,
        out_shape=out_shape,
        in_specs=in_specs,
        out_specs=jax.tree.map(lambda _: VMEM, out_shape),
        scratch_shapes=list(scratch),
        compiler_params=PARAMS,
        cost_estimate=pl.CostEstimate(flops=flops, bytes_accessed=bytes_accessed, transcendentals=0),
    )


def exchanged(block, first):
    count = lax.axis_size("pair")
    route = []
    for i in range(first, count - 1, 2):
        route += [(i, i + 1), (i + 1, i)]
    return lax.ppermute(block, "pair", route)


def per_device(inputs, cotangent, norm_gain, query_weight, key_weight, value_weight, output_weight):
    pair = lax.axis_index("pair").astype(jnp.int32).reshape(1)
    frames = lax.axis_size("pair") * PAIR
    piece, channels = inputs.shape[2:]
    rows, local = piece * SHARDS, query_weight.shape[1]
    x = inputs.reshape(piece, channels)
    cot = cotangent.reshape(piece, channels)
    gain = norm_gain
    wq, wk, wv, wo = query_weight.T, key_weight.T, value_weight.T, output_weight
    shape = jax.ShapeDtypeStruct
    wide = shape((rows, 2 * local), BF16)
    row_scratch = pltpu.VMEM((rows, channels), F32)
    near_scratch = pltpu.VMEM((3 * rows, 2 * local), F32)

    halves = call(
        norm_kernel,
        shape((PAIR, piece, channels), BF16),
        [pl.BlockSpec(memory_space=pl.ANY)] * 3,
        [
            pltpu.VMEM((piece, channels), BF16),
            pltpu.VMEM((piece, channels), BF16),
            pltpu.VMEM((channels,), BF16),
            pltpu.SemaphoreType.DMA((3,)),
        ],
    )(x, cot, gain)
    halves = lax.all_to_all(halves, "half", 0, 0)
    own_rows = shape((piece, channels), BF16)
    hidden, cot_rows = call(take_kernel, (own_rows, own_rows), [VMEM])(halves)
    hidden = lax.all_gather(hidden, "space", axis=0)
    b = call(key_value_kernel, wide, [VMEM] * 3, [row_scratch])(hidden, wk, wv)
    near = [exchanged(b, first) for first in (0, 1)]
    cot_rows = lax.all_gather(cot_rows, "space", axis=0)
    a = call(query_kernel, wide, [VMEM] * 4, [row_scratch])(hidden, cot_rows, wq, wo)
    *sends, own, small = call(
        functools.partial(attend_kernel, frames),
        (wide, wide, shape((rows, 2 * local), F32), shape((len(ORDERED), rows, 256), BF16)),
        [SMEM] + [VMEM] * 4,
        [near_scratch],
    )(pair, a, b, *near)
    arrived = [exchanged(send, first) for first, send in zip((0, 1), sends)]
    full = shape((rows, channels), F32)
    out, query_part = call(mix_kernel, (full, full), [SMEM] + [VMEM] * 6, [near_scratch])(
        pair, small, b, *near, wq, wo
    )
    parts = call(back_kernel, shape((PAIR * SHARDS, piece, channels), BF16), [VMEM] * 7, [row_scratch])(
        out, query_part, own, *arrived, wk, wv
    )
    parts = lax.all_to_all(parts, ("half", "space"), 0, 0)
    block, grads = call(
        finish_kernel, (shape((piece, channels), BF16), shape((piece, channels), BF16)), [VMEM] * 4
    )(x, cot, gain, parts)
    return block.reshape(inputs.shape), grads.reshape(inputs.shape)


def solution(mesh):
    devices = mesh.devices.reshape(-1, PAIR, SHARDS)
    mesh = Mesh(devices, ("pair", "half", "space"))
    frames = ("pair", "half")
    placed = (
        P(frames, None, "space", None),
        P(frames, None, "space", None),
        P(),
        P(None, "space"),
        P(None, "space"),
        P(None, "space"),
        P("space", None),
    )
    return jax.shard_map(
        per_device,
        mesh=mesh,
        in_specs=placed,
        out_specs=(P(frames, None, "space", None), P(frames, None, "space", None)),
        check_vma=False,
    )
```

```python
import functools

import jax
import jax.numpy as jnp
from jax import lax
from jax.experimental import pallas as pl
from jax.experimental.pallas import tpu as pltpu
from jax.sharding import Mesh
from jax.sharding import PartitionSpec as P

HEAD_DIM = 64
HEAD_SHIFT = 6
COST = 10_000_000_000
EPSILON = 1e-05
NEG_FILL = -1e30
ORDERED = (-2, -1, 0, 1, 2)
PAIR = 2
SHARDS = 4
BF16 = jnp.bfloat16
F32 = jnp.float32

VMEM = pl.BlockSpec(memory_space=pltpu.VMEM)
SMEM = pl.BlockSpec(memory_space=pltpu.SMEM)
PARAMS = pltpu.CompilerParams(vmem_limit_bytes=12 * 1024 * 1024)


def dot(a, b):
    return lax.dot_general(a, b, (((1,), (0,)), ((), ())), preferred_element_type=F32)


def dot_t(a, b):
    return lax.dot_general(a, b, (((1,), (1,)), ((), ())), preferred_element_type=F32)


def normalized(x):
    center = jnp.mean(x, axis=-1, keepdims=True)
    shifted = x - center
    spread = jnp.mean(jnp.square(shifted), axis=-1, keepdims=True)
    inverse = lax.rsqrt(spread + EPSILON)
    return shifted * inverse, inverse


def packed(block):
    width = block.shape[1] // 2
    return [block[:, :width], block[:, width:]]


def unpacked(block):
    rows = block.shape[0] // 2
    return jnp.concatenate([block[:rows], block[rows:]], axis=1)


def split_kernel(x_ref, cot_ref, out_ref):
    half = x_ref.shape[0] // PAIR
    x, cot = x_ref[...].astype(F32), cot_ref[...].astype(F32)
    for h in range(PAIR):
        rows = slice(h * half, (h + 1) * half)
        out_ref[h] = jnp.concatenate(packed(x[rows]) + packed(cot[rows]), axis=0).astype(BF16)


def norm_kernel(halves_ref, gain_ref, hidden_ref, cot_ref):
    half = halves_ref.shape[1] // 2
    both = [halves_ref[f].astype(F32) for f in range(PAIR)]
    x = jnp.concatenate([unpacked(v[:half]) for v in both], axis=0)
    normed, _ = normalized(x)
    hidden = normed * gain_ref[...].astype(F32).reshape(1, -1)
    rows = x.shape[0] // PAIR
    hidden = packed(hidden[:rows]) + packed(hidden[rows:])
    hidden_ref[...] = jnp.concatenate(hidden, axis=0).astype(BF16)
    cot_ref[...] = jnp.concatenate([v[half:] for v in both], axis=0).astype(BF16)


def gathered(g_ref, rows_ref):
    whole, width = g_ref.shape[1] // PAIR, g_ref.shape[2]
    half = whole // 2
    for frame in range(PAIR):
        for s in range(SHARDS):
            start = (frame * SHARDS + s) * half
            block = g_ref[s, frame * whole : (frame + 1) * whole].astype(F32)
            rows_ref[start : start + half, :width] = block[:half]
            rows_ref[start : start + half, width:] = block[half:]
    return rows_ref[...].astype(BF16)


def key_value_kernel(g_ref, wk_ref, wv_ref, b_ref, rows_ref):
    hidden = gathered(g_ref, rows_ref)
    keys = dot_t(hidden, wk_ref[...])
    vals = dot_t(hidden, wv_ref[...])
    b_ref[...] = jnp.concatenate([keys, vals], axis=1).astype(BF16)


def query_kernel(hidden_ref, cot_ref, wq_ref, wo_ref, a_ref, rows_ref):
    queries = dot_t(gathered(hidden_ref, rows_ref), wq_ref[...])
    out_grads = dot_t(gathered(cot_ref, rows_ref), wo_ref[...])
    a_ref[...] = jnp.concatenate([queries, out_grads], axis=1).astype(BF16)


def head_lanes(width, transposed=False):
    shape = (256, width) if transposed else (width, 256)
    lane = lax.broadcasted_iota(jnp.int32, shape, 1 if transposed else 0) >> HEAD_SHIFT
    col = lax.broadcasted_iota(jnp.int32, shape, 0 if transposed else 1)
    heads = (width >> HEAD_SHIFT) // 2
    want = jnp.where(lane < heads, lane, lane - heads + 128)
    return (col == want).astype(BF16)


def build_near(pair_ref, b_ref, even_ref, odd_ref, near_ref):
    rows = b_ref.shape[0]
    is_even = pair_ref[0] % 2 == 0
    from_even = even_ref[...].astype(F32)
    from_odd = odd_ref[...].astype(F32)
    near_ref[0:rows] = jnp.where(is_even, from_odd, from_even)
    near_ref[rows : 2 * rows] = b_ref[...].astype(F32)
    near_ref[2 * rows : 3 * rows] = jnp.where(is_even, from_even, from_odd)


def lane_scale(shape):
    lane = lax.broadcasted_iota(jnp.int32, shape, 1)
    return jnp.where(lane < shape[1] // 2, HEAD_DIM**-0.5, 1.0)


def attend_kernel(
    frames, pair_ref, a_ref, b_ref, even_ref, odd_ref, even_out, odd_out, own_ref, small_ref, near_ref
):
    pair = pair_ref[0]
    rows, width = a_ref.shape
    one = rows // PAIR
    build_near(pair_ref, b_ref, even_ref, odd_ref, near_ref)
    a = a_ref[...].astype(F32)
    reduce_mat = head_lanes(width)
    later = lax.broadcasted_iota(jnp.int32, (rows, 128), 0) >= one
    frame = pair * PAIR + later.astype(jnp.int32)
    scores, prob_grads = [], []
    for offset in ORDERED:
        start = (offset + 2) * one
        product = a * near_ref[start : start + rows]
        high = product.astype(BF16)
        low = (product - high.astype(F32)).astype(BF16)
        sums = dot(high, reduce_mat) + dot(low, reduce_mat)
        present = (frame + offset >= 0) & (frame + offset < frames)
        scores.append(jnp.where(present, sums[:, :128] * (HEAD_DIM**-0.5), NEG_FILL))
        prob_grads.append(sums[:, 128:])
    row_max = functools.reduce(jnp.maximum, scores)
    exponent = [jnp.exp(s - row_max) for s in scores]
    denominator = sum(exponent)
    attention = [e / denominator for e in exponent]
    row_delta = sum(p * g for p, g in zip(attention, prob_grads))
    scaled_a = a * lane_scale(a.shape)
    spread_mat = head_lanes(width, transposed=True)
    sent = []
    for i, (p, g) in enumerate(zip(attention, prob_grads)):
        score_grads = (p * (g - row_delta)).astype(BF16)
        small = jnp.concatenate([score_grads, p.astype(BF16)], axis=1)
        small_ref[i] = small
        sent.append(dot(small, spread_mat) * scaled_a)
    segments = []
    for i in range(len(ORDERED) + 1):
        terms = []
        if i < len(ORDERED):
            terms.append(sent[i][:one])
        if i > 0:
            terms.append(sent[i - 1][one:])
        segments.append(sum(terms))
    before = jnp.concatenate(segments[0:2], axis=0)
    after = jnp.concatenate(segments[4:6], axis=0)
    is_even = pair % 2 == 0
    even_out[...] = jnp.where(is_even, after, before).astype(BF16)
    odd_out[...] = jnp.where(is_even, before, after).astype(BF16)
    own_ref[0:one] = segments[2]
    own_ref[one:rows] = segments[3]


def mix_kernel(
    pair_ref, small_ref, b_ref, even_ref, odd_ref, wq_ref, wo_ref, out_ref, query_part_ref, near_ref
):
    build_near(pair_ref, b_ref, even_ref, odd_ref, near_ref)
    rows, width = b_ref.shape
    one, half = rows // PAIR, width // 2
    reduce_mat = head_lanes(width)
    mixed = jnp.zeros((rows, width), F32)
    for i in range(len(ORDERED)):
        mixed = mixed + dot_t(small_ref[i], reduce_mat) * near_ref[i * one : i * one + rows]
    mixed = (mixed * lane_scale(mixed.shape)).astype(BF16)
    query_part_ref[...] = dot(mixed[:, :half], wq_ref[...])
    out_ref[...] = dot(mixed[:, half:], wo_ref[...])


def back_kernel(out_ref, query_part_ref, own_ref, even_ref, odd_ref, wk_ref, wv_ref, parts_ref, rows_ref):
    width = own_ref.shape[1] // 2
    half = rows_ref.shape[0] // parts_ref.shape[0]
    total = own_ref[...] + even_ref[...].astype(F32) + odd_ref[...].astype(F32)
    total = total.astype(BF16)
    rows_ref[...] = (
        query_part_ref[...]
        + dot(total[:, :width], wk_ref[...])
        + dot(total[:, width:], wv_ref[...])
    )
    for part in range(PAIR * SHARDS):
        rows = slice(part * half, (part + 1) * half)
        both = packed(out_ref[rows]) + packed(rows_ref[rows])
        parts_ref[part] = jnp.concatenate(both, axis=0).astype(BF16)


def finish_kernel(x_ref, cot_ref, gain_ref, parts_ref, block_ref, grads_ref):
    half = parts_ref.shape[1] // 2
    summed = [
        sum(parts_ref[h * SHARDS + s].astype(F32) for s in range(SHARDS)) for h in range(PAIR)
    ]
    out = jnp.concatenate([unpacked(part[:half]) for part in summed], axis=0)
    hidden_grads = jnp.concatenate([unpacked(part[half:]) for part in summed], axis=0)
    x = x_ref[...].astype(F32)
    block_ref[...] = (x + out).astype(BF16)
    normed, inverse = normalized(x)
    scaled = hidden_grads * gain_ref[...].astype(F32).reshape(1, -1)
    layer_grads = inverse * (
        scaled
        - jnp.mean(scaled, axis=-1, keepdims=True)
        - normed * jnp.mean(scaled * normed, axis=-1, keepdims=True)
    )
    grads_ref[...] = (cot_ref[...].astype(F32) + layer_grads).astype(BF16)


def call(kernel, out_shape, in_specs, scratch=(), cost=0):
    return pl.pallas_call(
        kernel,
        out_shape=out_shape,
        in_specs=in_specs,
        out_specs=jax.tree.map(lambda _: VMEM, out_shape),
        scratch_shapes=list(scratch),
        compiler_params=PARAMS,
        cost_estimate=pl.CostEstimate(flops=cost, bytes_accessed=0, transcendentals=0),
    )


def exchanged(block, first):
    count = lax.axis_size("pair")
    route = []
    for i in range(first, count - 1, 2):
        route += [(i, i + 1), (i + 1, i)]
    return lax.ppermute(block, "pair", route)


def per_device(inputs, cotangent, norm_gain, query_weight, key_weight, value_weight, output_weight):
    pair = lax.axis_index("pair").astype(jnp.int32).reshape(1)
    frames = lax.axis_size("pair") * PAIR
    piece, channels = inputs.shape[2:]
    rows, local = piece * SHARDS, query_weight.shape[1]
    x = inputs.reshape(piece, channels)
    cot = cotangent.reshape(piece, channels)
    gain = norm_gain
    wq, wk, wv, wo = query_weight.T, key_weight.T, value_weight.T, output_weight
    shape = jax.ShapeDtypeStruct
    wide = shape((rows, 2 * local), BF16)
    row_scratch = pltpu.VMEM((rows, channels), F32)
    near_scratch = pltpu.VMEM((3 * rows, 2 * local), F32)

    packed_rows, packed_width = 2 * piece, channels // 2
    halves = call(split_kernel, shape((PAIR, packed_rows, packed_width), BF16), [VMEM] * 2, cost=COST)(x, cot)
    halves = lax.all_to_all(halves, "half", 0, 0)
    own_rows = shape((packed_rows, packed_width), BF16)
    hidden, cot_rows = call(norm_kernel, (own_rows, own_rows), [VMEM] * 2, cost=COST)(halves, gain)
    hidden = lax.all_gather(hidden, "space", axis=0)
    b = call(key_value_kernel, wide, [VMEM] * 3, [row_scratch])(hidden, wk, wv)
    near = [exchanged(b, first) for first in (0, 1)]
    cot_rows = lax.all_gather(cot_rows, "space", axis=0)
    a = call(query_kernel, wide, [VMEM] * 4, [row_scratch])(hidden, cot_rows, wq, wo)
    *sends, own, small = call(
        functools.partial(attend_kernel, frames),
        (wide, wide, shape((rows, 2 * local), F32), shape((len(ORDERED), rows, 256), BF16)),
        [SMEM] + [VMEM] * 4,
        [near_scratch],
    )(pair, a, b, *near)
    arrived = [exchanged(send, first) for first, send in zip((0, 1), sends)]
    full = shape((rows, channels), F32)
    out, query_part = call(mix_kernel, (full, full), [SMEM] + [VMEM] * 6, [near_scratch])(
        pair, small, b, *near, wq, wo
    )
    parts = call(back_kernel, shape((PAIR * SHARDS, packed_rows, packed_width), BF16), [VMEM] * 7, [row_scratch])(
        out, query_part, own, *arrived, wk, wv
    )
    parts = lax.all_to_all(parts, ("half", "space"), 0, 0)
    block, grads = call(
        finish_kernel, (shape((piece, channels), BF16), shape((piece, channels), BF16)), [VMEM] * 4
    )(x, cot, gain, parts)
    return block.reshape(inputs.shape), grads.reshape(inputs.shape)


def solution(mesh):
    devices = mesh.devices.reshape(-1, PAIR, SHARDS)
    mesh = Mesh(devices, ("pair", "half", "space"))
    frames = ("pair", "half")
    placed = (
        P(frames, None, "space", None),
        P(frames, None, "space", None),
        P(),
        P(None, "space"),
        P(None, "space"),
        P(None, "space"),
        P("space", None),
    )
    return jax.shard_map(
        per_device,
        mesh=mesh,
        in_specs=placed,
        out_specs=(P(frames, None, "space", None), P(frames, None, "space", None)),
        check_vma=False,
    )
```

```python
import functools

import jax
import jax.numpy as jnp
from jax import lax
from jax.experimental import pallas as pl
from jax.experimental.pallas import tpu as pltpu
from jax.sharding import Mesh
from jax.sharding import PartitionSpec as P

HEAD_DIM = 64
HEAD_SHIFT = 6
COST = 10_000_000_000
EPSILON = 1e-05
NEG_FILL = -1e30
ORDERED = (-2, -1, 0, 1, 2)
PAIR = 2
SHARDS = 4
BF16 = jnp.bfloat16
F32 = jnp.float32

VMEM = pl.BlockSpec(memory_space=pltpu.VMEM)
SMEM = pl.BlockSpec(memory_space=pltpu.SMEM)
PARAMS = pltpu.CompilerParams(vmem_limit_bytes=12 * 1024 * 1024)


def dot(a, b):
    return lax.dot_general(a, b, (((1,), (0,)), ((), ())), preferred_element_type=F32)


def dot_t(a, b):
    return lax.dot_general(a, b, (((1,), (1,)), ((), ())), preferred_element_type=F32)


def normalized(x):
    center = jnp.mean(x, axis=-1, keepdims=True)
    shifted = x - center
    spread = jnp.mean(jnp.square(shifted), axis=-1, keepdims=True)
    inverse = lax.rsqrt(spread + EPSILON)
    return shifted * inverse, inverse


def packed(block):
    width = block.shape[1] // 2
    return [block[:, :width], block[:, width:]]


def unpacked(block):
    rows = block.shape[0] // 2
    return jnp.concatenate([block[:rows], block[rows:]], axis=1)


def split_kernel(x_ref, cot_ref, out_ref):
    half = x_ref.shape[0] // PAIR
    x, cot = x_ref[...].astype(F32), cot_ref[...].astype(F32)
    for h in range(PAIR):
        rows = slice(h * half, (h + 1) * half)
        out_ref[h] = jnp.concatenate(packed(x[rows]) + packed(cot[rows]), axis=0).astype(BF16)


def norm_kernel(halves_ref, gain_ref, hidden_ref, cot_ref):
    half = halves_ref.shape[1] // 2
    both = [halves_ref[f].astype(F32) for f in range(PAIR)]
    x = jnp.concatenate([unpacked(v[:half]) for v in both], axis=0)
    normed, _ = normalized(x)
    hidden = normed * gain_ref[...].astype(F32).reshape(1, -1)
    rows = x.shape[0] // PAIR
    hidden = packed(hidden[:rows]) + packed(hidden[rows:])
    hidden_ref[...] = jnp.concatenate(hidden, axis=0).astype(BF16)
    cot_ref[...] = jnp.concatenate([v[half:] for v in both], axis=0).astype(BF16)


def gathered(g_ref, rows_ref):
    whole, width = g_ref.shape[1] // PAIR, g_ref.shape[2]
    half = whole // 2
    for frame in range(PAIR):
        for s in range(SHARDS):
            start = (frame * SHARDS + s) * half
            block = g_ref[s, frame * whole : (frame + 1) * whole].astype(F32)
            rows_ref[start : start + half, :width] = block[:half]
            rows_ref[start : start + half, width:] = block[half:]
    return rows_ref[...].astype(BF16)


def key_value_kernel(g_ref, wk_ref, wv_ref, b_ref, rows_ref):
    hidden = gathered(g_ref, rows_ref)
    keys = dot_t(hidden, wk_ref[...])
    vals = dot_t(hidden, wv_ref[...])
    b_ref[...] = jnp.concatenate([keys, vals], axis=1).astype(BF16)


def query_kernel(hidden_ref, cot_ref, wq_ref, wo_ref, a_ref, rows_ref):
    queries = dot_t(gathered(hidden_ref, rows_ref), wq_ref[...])
    out_grads = dot_t(gathered(cot_ref, rows_ref), wo_ref[...])
    a_ref[...] = jnp.concatenate([queries, out_grads], axis=1).astype(BF16)


def head_lanes(width, transposed=False):
    shape = (256, width) if transposed else (width, 256)
    lane = lax.broadcasted_iota(jnp.int32, shape, 1 if transposed else 0) >> HEAD_SHIFT
    col = lax.broadcasted_iota(jnp.int32, shape, 0 if transposed else 1)
    heads = (width >> HEAD_SHIFT) // 2
    want = jnp.where(lane < heads, lane, lane - heads + 128)
    return (col == want).astype(BF16)


def build_near(pair_ref, b_ref, even_ref, odd_ref, near_ref):
    rows = b_ref.shape[0]
    is_even = pair_ref[0] % 2 == 0
    from_even = even_ref[...].astype(F32)
    from_odd = odd_ref[...].astype(F32)
    near_ref[0:rows] = jnp.where(is_even, from_odd, from_even)
    near_ref[rows : 2 * rows] = b_ref[...].astype(F32)
    near_ref[2 * rows : 3 * rows] = jnp.where(is_even, from_even, from_odd)


def lane_scale(shape):
    lane = lax.broadcasted_iota(jnp.int32, shape, 1)
    return jnp.where(lane < shape[1] // 2, HEAD_DIM**-0.5, 1.0)


def attend_kernel(
    frames, pair_ref, a_ref, b_ref, even_ref, odd_ref, even_out, odd_out, own_ref, small_ref, near_ref
):
    pair = pair_ref[0]
    rows, width = a_ref.shape
    one = rows // PAIR
    build_near(pair_ref, b_ref, even_ref, odd_ref, near_ref)
    a = a_ref[...].astype(F32)
    reduce_mat = head_lanes(width)
    later = lax.broadcasted_iota(jnp.int32, (rows, 128), 0) >= one
    frame = pair * PAIR + later.astype(jnp.int32)
    scores, prob_grads = [], []
    for offset in ORDERED:
        start = (offset + 2) * one
        product = a * near_ref[start : start + rows]
        high = product.astype(BF16)
        low = (product - high.astype(F32)).astype(BF16)
        sums = dot(high, reduce_mat) + dot(low, reduce_mat)
        present = (frame + offset >= 0) & (frame + offset < frames)
        scores.append(jnp.where(present, sums[:, :128] * (HEAD_DIM**-0.5), NEG_FILL))
        prob_grads.append(sums[:, 128:])
    row_max = functools.reduce(jnp.maximum, scores)
    exponent = [jnp.exp(s - row_max) for s in scores]
    denominator = sum(exponent)
    attention = [e / denominator for e in exponent]
    row_delta = sum(p * g for p, g in zip(attention, prob_grads))
    scaled_a = a * lane_scale(a.shape)
    spread_mat = head_lanes(width, transposed=True)
    sent = []
    for i, (p, g) in enumerate(zip(attention, prob_grads)):
        score_grads = (p * (g - row_delta)).astype(BF16)
        small = jnp.concatenate([score_grads, p.astype(BF16)], axis=1)
        small_ref[i] = small
        sent.append(dot(small, spread_mat) * scaled_a)
    segments = []
    for i in range(len(ORDERED) + 1):
        terms = []
        if i < len(ORDERED):
            terms.append(sent[i][:one])
        if i > 0:
            terms.append(sent[i - 1][one:])
        segments.append(sum(terms))
    before = jnp.concatenate(segments[0:2], axis=0)
    after = jnp.concatenate(segments[4:6], axis=0)
    is_even = pair % 2 == 0
    even_out[...] = jnp.where(is_even, after, before).astype(BF16)
    odd_out[...] = jnp.where(is_even, before, after).astype(BF16)
    own_ref[0:one] = segments[2]
    own_ref[one:rows] = segments[3]


def mix_kernel(
    pair_ref, small_ref, b_ref, even_ref, odd_ref, wq_ref, wo_ref, out_ref, query_part_ref, near_ref
):
    build_near(pair_ref, b_ref, even_ref, odd_ref, near_ref)
    rows, width = b_ref.shape
    one, half = rows // PAIR, width // 2
    reduce_mat = head_lanes(width)
    mixed = jnp.zeros((rows, width), F32)
    for i in range(len(ORDERED)):
        mixed = mixed + dot_t(small_ref[i], reduce_mat) * near_ref[i * one : i * one + rows]
    mixed = (mixed * lane_scale(mixed.shape)).astype(BF16)
    query_part_ref[...] = dot(mixed[:, :half], wq_ref[...])
    out_ref[...] = dot(mixed[:, half:], wo_ref[...]).astype(BF16)


def join_kernel(core_ref, both_ref, out_ref, sum_ref):
    sum_ref[...] = both_ref[0].astype(F32) + both_ref[1].astype(F32)
    second = core_ref[0] == 1
    share = out_ref.shape[0] // (PAIR * SHARDS)
    for part in range(PAIR * SHARDS):
        start = part * 2 * share
        out_ref[part * share : (part + 1) * share] = jnp.where(
            second, sum_ref[start + share : start + 2 * share], sum_ref[start : start + share]
        )


def back_kernel(out_ref, query_part_ref, own_ref, odd_ref, even_ref, wk_ref, wv_ref, parts_ref, rows_ref):
    width = own_ref.shape[1] // 2
    half = rows_ref.shape[0] // parts_ref.shape[0]
    share = half // 2
    total = own_ref[...] + even_ref[...].astype(F32) + odd_ref[...].astype(F32)
    total = total.astype(BF16)
    rows_ref[...] = (
        query_part_ref[...]
        + dot(total[:, :width], wk_ref[...])
        + dot(total[:, width:], wv_ref[...])
    )
    for part in range(PAIR * SHARDS):
        grads = rows_ref[part * half : (part + 1) * half]
        out = out_ref[part * share : (part + 1) * share]
        parts_ref[part] = jnp.concatenate(packed(grads) + packed(out), axis=0).astype(BF16)


def finish_kernel(x_ref, cot_ref, gain_ref, parts_ref, block_ref, grads_ref):
    rows = x_ref.shape[0]
    out, hidden_grads = [], []
    for h in range(PAIR):
        parts = [parts_ref[h * SHARDS + s].astype(F32) for s in range(SHARDS)]
        hidden_grads.append(unpacked(sum(part[:rows] for part in parts)))
        for core in range(2):
            out.append(unpacked(sum(part[rows:] for part in parts[core::2])))
    out = jnp.concatenate(out, axis=0)
    hidden_grads = jnp.concatenate(hidden_grads, axis=0)
    x = x_ref[...].astype(F32)
    block_ref[...] = (x + out).astype(BF16)
    normed, inverse = normalized(x)
    scaled = hidden_grads * gain_ref[...].astype(F32).reshape(1, -1)
    layer_grads = inverse * (
        scaled
        - jnp.mean(scaled, axis=-1, keepdims=True)
        - normed * jnp.mean(scaled * normed, axis=-1, keepdims=True)
    )
    grads_ref[...] = (cot_ref[...].astype(F32) + layer_grads).astype(BF16)


def call(kernel, out_shape, in_specs, scratch=(), cost=0):
    return pl.pallas_call(
        kernel,
        out_shape=out_shape,
        in_specs=in_specs,
        out_specs=jax.tree.map(lambda _: VMEM, out_shape),
        scratch_shapes=list(scratch),
        compiler_params=PARAMS,
        cost_estimate=pl.CostEstimate(flops=cost, bytes_accessed=0, transcendentals=0),
    )


def exchanged(block, first):
    count = lax.axis_size("pair")
    route = []
    for i in range(first, count - 1, 2):
        route += [(i, i + 1), (i + 1, i)]
    return lax.ppermute(block, "pair", route)


def per_device(inputs, cotangent, norm_gain, query_weight, key_weight, value_weight, output_weight):
    pair = lax.axis_index("pair").astype(jnp.int32).reshape(1)
    frames = lax.axis_size("pair") * PAIR
    piece, channels = inputs.shape[2:]
    rows, local = piece * SHARDS, query_weight.shape[1]
    x = inputs.reshape(piece, channels)
    cot = cotangent.reshape(piece, channels)
    gain = norm_gain
    wq, wk, wv, wo = query_weight.T, key_weight.T, value_weight.T, output_weight
    shape = jax.ShapeDtypeStruct
    wide = shape((rows, 2 * local), BF16)
    row_scratch = pltpu.VMEM((rows, channels), F32)
    near_scratch = pltpu.VMEM((3 * rows, 2 * local), F32)

    packed_rows, packed_width = 2 * piece, channels // 2
    halves = call(split_kernel, shape((PAIR, packed_rows, packed_width), BF16), [VMEM] * 2, cost=COST)(x, cot)
    halves = lax.all_to_all(halves, "half", 0, 0)
    own_rows = shape((packed_rows, packed_width), BF16)
    hidden, cot_rows = call(norm_kernel, (own_rows, own_rows), [VMEM] * 2, cost=COST)(halves, gain)
    hidden = lax.all_gather(hidden, "space", axis=0)
    b = call(key_value_kernel, wide, [VMEM] * 3, [row_scratch])(hidden, wk, wv)
    near = [exchanged(b, first) for first in (0, 1)]
    cot_rows = lax.all_gather(cot_rows, "space", axis=0)
    a = call(query_kernel, wide, [VMEM] * 4, [row_scratch])(hidden, cot_rows, wq, wo)
    *sends, own, small = call(
        functools.partial(attend_kernel, frames),
        (wide, wide, shape((rows, 2 * local), F32), shape((len(ORDERED), rows, 256), BF16)),
        [SMEM] + [VMEM] * 4,
        [near_scratch],
    )(pair, a, b, *near)
    arrived = [exchanged(sends[first], first) for first in (1, 0)]
    out, query_part = call(
        mix_kernel,
        (shape((rows, channels), BF16), shape((rows, channels), F32)),
        [SMEM] + [VMEM] * 6,
        [near_scratch],
    )(pair, small, b, *near, wq, wo)
    cores = [[s, s + 1] for s in range(0, SHARDS, 2)]
    out = lax.all_gather(out, "space", axis=0, axis_index_groups=cores)
    core = (lax.axis_index("space") % 2).astype(jnp.int32).reshape(1)
    out = call(join_kernel, shape((rows // 2, channels), F32), [SMEM, VMEM], [row_scratch])(core, out)
    parts = call(
        back_kernel,
        shape((PAIR * SHARDS, packed_rows // PAIR + piece // 2, packed_width), BF16),
        [VMEM] * 7,
        [row_scratch],
    )(out, query_part, own, *arrived, wk, wv)
    parts = lax.all_to_all(parts, ("half", "space"), 0, 0)
    block, grads = call(
        finish_kernel, (shape((piece, channels), BF16), shape((piece, channels), BF16)), [VMEM] * 4
    )(x, cot, gain, parts)
    return block.reshape(inputs.shape), grads.reshape(inputs.shape)


def solution(mesh):
    devices = mesh.devices.reshape(-1, PAIR, SHARDS)
    mesh = Mesh(devices, ("pair", "half", "space"))
    frames = ("pair", "half")
    placed = (
        P(frames, None, "space", None),
        P(frames, None, "space", None),
        P(),
        P(None, "space"),
        P(None, "space"),
        P(None, "space"),
        P("space", None),
    )
    return jax.shard_map(
        per_device,
        mesh=mesh,
        in_specs=placed,
        out_specs=(P(frames, None, "space", None), P(frames, None, "space", None)),
        check_vma=False,
    )
```

```python
import functools

import jax
import jax.numpy as jnp
from jax import lax
from jax.experimental import pallas as pl
from jax.experimental.pallas import tpu as pltpu
from jax.sharding import Mesh
from jax.sharding import PartitionSpec as P

HEAD_DIM = 64
HEAD_SHIFT = 6
COST = 10_000_000_000
EPSILON = 1e-05
NEG_FILL = -1e30
ORDERED = (-2, -1, 0, 1, 2)
PAIR = 2
SHARDS = 4
BF16 = jnp.bfloat16
F32 = jnp.float32

VMEM = pl.BlockSpec(memory_space=pltpu.VMEM)
SMEM = pl.BlockSpec(memory_space=pltpu.SMEM)
PARAMS = pltpu.CompilerParams(vmem_limit_bytes=12 * 1024 * 1024)


def dot(a, b):
    return lax.dot_general(a, b, (((1,), (0,)), ((), ())), preferred_element_type=F32)


def dot_t(a, b):
    return lax.dot_general(a, b, (((1,), (1,)), ((), ())), preferred_element_type=F32)


def normalized(x):
    center = jnp.mean(x, axis=-1, keepdims=True)
    shifted = x - center
    spread = jnp.mean(jnp.square(shifted), axis=-1, keepdims=True)
    inverse = lax.rsqrt(spread + EPSILON)
    return shifted * inverse, inverse


def packed(block):
    width = block.shape[1] // 2
    return [block[:, :width], block[:, width:]]


def unpacked(block):
    rows = block.shape[0] // 2
    return jnp.concatenate([block[:rows], block[rows:]], axis=1)


def norm_kernel(halves_ref, gain_ref, hidden_ref, cot_ref):
    half = halves_ref.shape[1] // 2
    both = [halves_ref[f].astype(F32) for f in range(PAIR)]
    x = jnp.concatenate([v[:half] for v in both], axis=0)
    normed, _ = normalized(x)
    hidden = normed * gain_ref[...].astype(F32).reshape(1, -1)
    rows = x.shape[0] // PAIR
    hidden = packed(hidden[:rows]) + packed(hidden[rows:])
    hidden_ref[...] = jnp.concatenate(hidden, axis=0).astype(BF16)
    cot = packed(both[0][half:]) + packed(both[1][half:])
    cot_ref[...] = jnp.concatenate(cot, axis=0).astype(BF16)


def gathered(g_ref, rows_ref):
    whole, width = g_ref.shape[1] // PAIR, g_ref.shape[2]
    half = whole // 2
    for frame in range(PAIR):
        for s in range(SHARDS):
            start = (frame * SHARDS + s) * half
            block = g_ref[s, frame * whole : (frame + 1) * whole].astype(F32)
            rows_ref[start : start + half, :width] = block[:half]
            rows_ref[start : start + half, width:] = block[half:]
    return rows_ref[...].astype(BF16)


def key_value_kernel(g_ref, wk_ref, wv_ref, b_ref, rows_ref):
    hidden = gathered(g_ref, rows_ref)
    keys = dot_t(hidden, wk_ref[...])
    vals = dot_t(hidden, wv_ref[...])
    b_ref[...] = jnp.concatenate([keys, vals], axis=1).astype(BF16)


def query_kernel(hidden_ref, cot_ref, wq_ref, wo_ref, a_ref, rows_ref):
    queries = dot_t(gathered(hidden_ref, rows_ref), wq_ref[...])
    out_grads = dot_t(gathered(cot_ref, rows_ref), wo_ref[...])
    a_ref[...] = jnp.concatenate([queries, out_grads], axis=1).astype(BF16)


def head_lanes(width, transposed=False):
    shape = (256, width) if transposed else (width, 256)
    lane = lax.broadcasted_iota(jnp.int32, shape, 1 if transposed else 0) >> HEAD_SHIFT
    col = lax.broadcasted_iota(jnp.int32, shape, 0 if transposed else 1)
    heads = (width >> HEAD_SHIFT) // 2
    want = jnp.where(lane < heads, lane, lane - heads + 128)
    return (col == want).astype(BF16)


def build_near(pair_ref, b_ref, even_ref, odd_ref, near_ref):
    rows = b_ref.shape[0]
    is_even = pair_ref[0] % 2 == 0
    from_even = even_ref[...].astype(F32)
    from_odd = odd_ref[...].astype(F32)
    near_ref[0:rows] = jnp.where(is_even, from_odd, from_even)
    near_ref[rows : 2 * rows] = b_ref[...].astype(F32)
    near_ref[2 * rows : 3 * rows] = jnp.where(is_even, from_even, from_odd)


def lane_scale(shape):
    lane = lax.broadcasted_iota(jnp.int32, shape, 1)
    return jnp.where(lane < shape[1] // 2, HEAD_DIM**-0.5, 1.0)


def attend_kernel(
    frames, pair_ref, a_ref, b_ref, even_ref, odd_ref, even_out, odd_out, own_ref, small_ref, near_ref
):
    pair = pair_ref[0]
    rows, width = a_ref.shape
    one = rows // PAIR
    build_near(pair_ref, b_ref, even_ref, odd_ref, near_ref)
    a = a_ref[...].astype(F32)
    reduce_mat = head_lanes(width)
    later = lax.broadcasted_iota(jnp.int32, (rows, 128), 0) >= one
    frame = pair * PAIR + later.astype(jnp.int32)
    scores, prob_grads = [], []
    for offset in ORDERED:
        start = (offset + 2) * one
        product = a * near_ref[start : start + rows]
        high = product.astype(BF16)
        low = (product - high.astype(F32)).astype(BF16)
        sums = dot(high, reduce_mat) + dot(low, reduce_mat)
        present = (frame + offset >= 0) & (frame + offset < frames)
        scores.append(jnp.where(present, sums[:, :128] * (HEAD_DIM**-0.5), NEG_FILL))
        prob_grads.append(sums[:, 128:])
    row_max = functools.reduce(jnp.maximum, scores)
    exponent = [jnp.exp(s - row_max) for s in scores]
    denominator = sum(exponent)
    attention = [e / denominator for e in exponent]
    row_delta = sum(p * g for p, g in zip(attention, prob_grads))
    scaled_a = a * lane_scale(a.shape)
    spread_mat = head_lanes(width, transposed=True)
    sent = []
    for i, (p, g) in enumerate(zip(attention, prob_grads)):
        score_grads = (p * (g - row_delta)).astype(BF16)
        small = jnp.concatenate([score_grads, p.astype(BF16)], axis=1)
        small_ref[i] = small
        sent.append(dot(small, spread_mat) * scaled_a)
    segments = []
    for i in range(len(ORDERED) + 1):
        terms = []
        if i < len(ORDERED):
            terms.append(sent[i][:one])
        if i > 0:
            terms.append(sent[i - 1][one:])
        segments.append(sum(terms))
    before = jnp.concatenate(segments[0:2], axis=0)
    after = jnp.concatenate(segments[4:6], axis=0)
    is_even = pair % 2 == 0
    even_out[...] = jnp.where(is_even, after, before).astype(BF16)
    odd_out[...] = jnp.where(is_even, before, after).astype(BF16)
    own_ref[0:one] = segments[2]
    own_ref[one:rows] = segments[3]


def mix_kernel(
    pair_ref, small_ref, b_ref, even_ref, odd_ref, wq_ref, wo_ref, out_ref, query_part_ref, near_ref
):
    build_near(pair_ref, b_ref, even_ref, odd_ref, near_ref)
    rows, width = b_ref.shape
    one, half = rows // PAIR, width // 2
    reduce_mat = head_lanes(width)
    mixed = jnp.zeros((rows, width), F32)
    for i in range(len(ORDERED)):
        mixed = mixed + dot_t(small_ref[i], reduce_mat) * near_ref[i * one : i * one + rows]
    mixed = (mixed * lane_scale(mixed.shape)).astype(BF16)
    query_part_ref[...] = dot(mixed[:, :half], wq_ref[...])
    out_ref[...] = dot(mixed[:, half:], wo_ref[...]).astype(BF16)


def join_kernel(core_ref, both_ref, out_ref, sum_ref):
    sum_ref[...] = both_ref[0].astype(F32) + both_ref[1].astype(F32)
    second = core_ref[0] == 1
    share = out_ref.shape[0] // (PAIR * SHARDS)
    for part in range(PAIR * SHARDS):
        start = part * 2 * share
        out_ref[part * share : (part + 1) * share] = jnp.where(
            second, sum_ref[start + share : start + 2 * share], sum_ref[start : start + share]
        )


def back_kernel(out_ref, query_part_ref, own_ref, odd_ref, even_ref, wk_ref, wv_ref, parts_ref, rows_ref):
    width = own_ref.shape[1] // 2
    half = rows_ref.shape[0] // parts_ref.shape[0]
    share = half // 2
    total = own_ref[...] + even_ref[...].astype(F32) + odd_ref[...].astype(F32)
    total = total.astype(BF16)
    rows_ref[...] = (
        query_part_ref[...]
        + dot(total[:, :width], wk_ref[...])
        + dot(total[:, width:], wv_ref[...])
    )
    for part in range(PAIR * SHARDS):
        grads = rows_ref[part * half : (part + 1) * half]
        out = out_ref[part * share : (part + 1) * share]
        parts_ref[part] = jnp.concatenate(packed(grads) + packed(out), axis=0).astype(BF16)


def finish_kernel(x_ref, cot_ref, gain_ref, parts_ref, block_ref, grads_ref):
    rows = x_ref.shape[0]
    out, hidden_grads = [], []
    for h in range(PAIR):
        parts = [parts_ref[h * SHARDS + s].astype(F32) for s in range(SHARDS)]
        hidden_grads.append(unpacked(sum(part[:rows] for part in parts)))
        for core in range(2):
            out.append(unpacked(sum(part[rows:] for part in parts[core::2])))
    out = jnp.concatenate(out, axis=0)
    hidden_grads = jnp.concatenate(hidden_grads, axis=0)
    x = x_ref[...].astype(F32)
    block_ref[...] = (x + out).astype(BF16)
    normed, inverse = normalized(x)
    scaled = hidden_grads * gain_ref[...].astype(F32).reshape(1, -1)
    layer_grads = inverse * (
        scaled
        - jnp.mean(scaled, axis=-1, keepdims=True)
        - normed * jnp.mean(scaled * normed, axis=-1, keepdims=True)
    )
    grads_ref[...] = (cot_ref[...].astype(F32) + layer_grads).astype(BF16)


def call(kernel, out_shape, in_specs, scratch=(), cost=0):
    return pl.pallas_call(
        kernel,
        out_shape=out_shape,
        in_specs=in_specs,
        out_specs=jax.tree.map(lambda _: VMEM, out_shape),
        scratch_shapes=list(scratch),
        compiler_params=PARAMS,
        cost_estimate=pl.CostEstimate(flops=cost, bytes_accessed=0, transcendentals=0),
    )


def exchanged(block, first):
    count = lax.axis_size("pair")
    route = []
    for i in range(first, count - 1, 2):
        route += [(i, i + 1), (i + 1, i)]
    return lax.ppermute(block, "pair", route)


def per_device(inputs, cotangent, norm_gain, query_weight, key_weight, value_weight, output_weight):
    pair = lax.axis_index("pair").astype(jnp.int32).reshape(1)
    frames = lax.axis_size("pair") * PAIR
    piece, channels = inputs.shape[2:]
    rows, local = piece * SHARDS, query_weight.shape[1]
    x = inputs.reshape(piece, channels)
    cot = cotangent.reshape(piece, channels)
    gain = norm_gain
    wq, wk, wv, wo = query_weight.T, key_weight.T, value_weight.T, output_weight
    shape = jax.ShapeDtypeStruct
    wide = shape((rows, 2 * local), BF16)
    row_scratch = pltpu.VMEM((rows, channels), F32)
    near_scratch = pltpu.VMEM((3 * rows, 2 * local), F32)

    packed_rows, packed_width = 2 * piece, channels // 2
    halves = [block.reshape(PAIR, piece // PAIR, channels) for block in (x, cot)]
    halves = jnp.concatenate(halves, axis=1)
    halves = lax.all_to_all(halves, "half", 0, 0)
    own_rows = shape((packed_rows, packed_width), BF16)
    hidden, cot_rows = call(norm_kernel, (own_rows, own_rows), [VMEM] * 2, cost=COST)(halves, gain)
    hidden = lax.all_gather(hidden, "space", axis=0)
    b = call(key_value_kernel, wide, [VMEM] * 3, [row_scratch])(hidden, wk, wv)
    near = [exchanged(b, first) for first in (0, 1)]
    cot_rows = lax.all_gather(cot_rows, "space", axis=0)
    a = call(query_kernel, wide, [VMEM] * 4, [row_scratch])(hidden, cot_rows, wq, wo)
    *sends, own, small = call(
        functools.partial(attend_kernel, frames),
        (wide, wide, shape((rows, 2 * local), F32), shape((len(ORDERED), rows, 256), BF16)),
        [SMEM] + [VMEM] * 4,
        [near_scratch],
    )(pair, a, b, *near)
    arrived = [exchanged(sends[first], first) for first in (1, 0)]
    out, query_part = call(
        mix_kernel,
        (shape((rows, channels), BF16), shape((rows, channels), F32)),
        [SMEM] + [VMEM] * 6,
        [near_scratch],
    )(pair, small, b, *near, wq, wo)
    cores = [[s, s + 1] for s in range(0, SHARDS, 2)]
    out = lax.all_gather(out, "space", axis=0, axis_index_groups=cores)
    core = (lax.axis_index("space") % 2).astype(jnp.int32).reshape(1)
    out = call(join_kernel, shape((rows // 2, channels), F32), [SMEM, VMEM], [row_scratch])(core, out)
    parts = call(
        back_kernel,
        shape((PAIR * SHARDS, packed_rows // PAIR + piece // 2, packed_width), BF16),
        [VMEM] * 7,
        [row_scratch],
    )(out, query_part, own, *arrived, wk, wv)
    parts = lax.all_to_all(parts, ("half", "space"), 0, 0)
    block, grads = call(
        finish_kernel, (shape((piece, channels), BF16), shape((piece, channels), BF16)), [VMEM] * 4
    )(x, cot, gain, parts)
    return block.reshape(inputs.shape), grads.reshape(inputs.shape)


def solution(mesh):
    devices = mesh.devices.reshape(-1, PAIR, SHARDS)
    mesh = Mesh(devices, ("pair", "half", "space"))
    frames = ("pair", "half")
    placed = (
        P(frames, None, "space", None),
        P(frames, None, "space", None),
        P(),
        P(None, "space"),
        P(None, "space"),
        P(None, "space"),
        P("space", None),
    )
    return jax.shard_map(
        per_device,
        mesh=mesh,
        in_specs=placed,
        out_specs=(P(frames, None, "space", None), P(frames, None, "space", None)),
        check_vma=False,
    )
```

```python
import functools

import jax
import jax.numpy as jnp
from jax import lax
from jax.experimental import pallas as pl
from jax.experimental.pallas import tpu as pltpu
from jax.sharding import Mesh
from jax.sharding import PartitionSpec as P

HEAD_DIM = 64
HEAD_SHIFT = 6
COST = 10_000_000_000
EPSILON = 1e-05
NEG_FILL = -1e30
ORDERED = (-2, -1, 0, 1, 2)
PAIR = 2
SHARDS = 4
BF16 = jnp.bfloat16
F32 = jnp.float32

VMEM = pl.BlockSpec(memory_space=pltpu.VMEM)
SMEM = pl.BlockSpec(memory_space=pltpu.SMEM)
PARAMS = pltpu.CompilerParams(vmem_limit_bytes=12 * 1024 * 1024)


def dot(a, b):
    return lax.dot_general(a, b, (((1,), (0,)), ((), ())), preferred_element_type=F32)


def dot_t(a, b):
    return lax.dot_general(a, b, (((1,), (1,)), ((), ())), preferred_element_type=F32)


def normalized(x):
    center = jnp.mean(x, axis=-1, keepdims=True)
    shifted = x - center
    spread = jnp.mean(jnp.square(shifted), axis=-1, keepdims=True)
    inverse = lax.rsqrt(spread + EPSILON)
    return shifted * inverse, inverse


def packed(block):
    width = block.shape[1] // 2
    return [block[:, :width], block[:, width:]]


def unpacked(block):
    rows = block.shape[0] // 2
    return jnp.concatenate([block[:rows], block[rows:]], axis=1)


def norm_kernel(halves_ref, gain_ref, hidden_ref, cot_ref):
    half = halves_ref.shape[1] // 2
    both = [halves_ref[f].astype(F32) for f in range(PAIR)]
    x = jnp.concatenate([v[:half] for v in both], axis=0)
    normed, _ = normalized(x)
    hidden = normed * gain_ref[...].astype(F32).reshape(1, -1)
    rows = x.shape[0] // PAIR
    hidden = packed(hidden[:rows]) + packed(hidden[rows:])
    hidden_ref[...] = jnp.concatenate(hidden, axis=0).astype(BF16)
    cot = packed(both[0][half:]) + packed(both[1][half:])
    cot_ref[...] = jnp.concatenate(cot, axis=0).astype(BF16)


def gathered(g_ref, rows_ref):
    whole, width = g_ref.shape[1] // PAIR, g_ref.shape[2]
    half = whole // 2
    for s in range(SHARDS):
        blocks = g_ref[s].astype(F32)
        for frame in range(PAIR):
            start = (frame * SHARDS + s) * half
            block = blocks[frame * whole : (frame + 1) * whole]
            rows_ref[start : start + half, :width] = block[:half]
            rows_ref[start : start + half, width:] = block[half:]
    return rows_ref[...].astype(BF16)


def key_value_kernel(g_ref, wk_ref, wv_ref, b_ref, rows_ref):
    hidden = gathered(g_ref, rows_ref)
    keys = dot_t(hidden, wk_ref[...])
    vals = dot_t(hidden, wv_ref[...])
    b_ref[...] = jnp.concatenate([keys, vals], axis=1).astype(BF16)


def query_kernel(hidden_ref, cot_ref, wq_ref, wo_ref, a_ref, rows_ref):
    queries = dot_t(gathered(hidden_ref, rows_ref), wq_ref[...])
    out_grads = dot_t(gathered(cot_ref, rows_ref), wo_ref[...])
    a_ref[...] = jnp.concatenate([queries, out_grads], axis=1).astype(BF16)


def head_lanes(width, transposed=False):
    shape = (256, width) if transposed else (width, 256)
    lane = lax.broadcasted_iota(jnp.int32, shape, 1 if transposed else 0) >> HEAD_SHIFT
    col = lax.broadcasted_iota(jnp.int32, shape, 0 if transposed else 1)
    heads = (width >> HEAD_SHIFT) // 2
    want = jnp.where(lane < heads, lane, lane - heads + 128)
    return (col == want).astype(BF16)


def build_near(pair_ref, b_ref, even_ref, odd_ref, near_ref):
    rows = b_ref.shape[0]
    is_even = pair_ref[0] % 2 == 0
    from_even = even_ref[...].astype(F32)
    from_odd = odd_ref[...].astype(F32)
    near_ref[0:rows] = jnp.where(is_even, from_odd, from_even)
    near_ref[rows : 2 * rows] = b_ref[...].astype(F32)
    near_ref[2 * rows : 3 * rows] = jnp.where(is_even, from_even, from_odd)


def lane_scale(shape):
    lane = lax.broadcasted_iota(jnp.int32, shape, 1)
    return jnp.where(lane < shape[1] // 2, HEAD_DIM**-0.5, 1.0)


def attend_kernel(
    frames, pair_ref, a_ref, b_ref, even_ref, odd_ref, even_out, odd_out, own_ref, small_ref, near_ref
):
    pair = pair_ref[0]
    rows, width = a_ref.shape
    one = rows // PAIR
    build_near(pair_ref, b_ref, even_ref, odd_ref, near_ref)
    a = a_ref[...].astype(F32)
    reduce_mat = head_lanes(width)
    later = lax.broadcasted_iota(jnp.int32, (rows, 128), 0) >= one
    frame = pair * PAIR + later.astype(jnp.int32)
    scores, prob_grads = [], []
    for offset in ORDERED:
        start = (offset + 2) * one
        product = a * near_ref[start : start + rows]
        high = product.astype(BF16)
        low = (product - high.astype(F32)).astype(BF16)
        sums = dot(high, reduce_mat) + dot(low, reduce_mat)
        present = (frame + offset >= 0) & (frame + offset < frames)
        scores.append(jnp.where(present, sums[:, :128] * (HEAD_DIM**-0.5), NEG_FILL))
        prob_grads.append(sums[:, 128:])
    row_max = functools.reduce(jnp.maximum, scores)
    exponent = [jnp.exp(s - row_max) for s in scores]
    denominator = sum(exponent)
    attention = [e / denominator for e in exponent]
    row_delta = sum(p * g for p, g in zip(attention, prob_grads))
    scaled_a = a * lane_scale(a.shape)
    spread_mat = head_lanes(width, transposed=True)
    sent = []
    for i, (p, g) in enumerate(zip(attention, prob_grads)):
        score_grads = (p * (g - row_delta)).astype(BF16)
        small = jnp.concatenate([score_grads, p.astype(BF16)], axis=1)
        small_ref[i] = small
        sent.append(dot(small, spread_mat) * scaled_a)
    segments = []
    for i in range(len(ORDERED) + 1):
        terms = []
        if i < len(ORDERED):
            terms.append(sent[i][:one])
        if i > 0:
            terms.append(sent[i - 1][one:])
        segments.append(sum(terms))
    before = jnp.concatenate(segments[0:2], axis=0)
    after = jnp.concatenate(segments[4:6], axis=0)
    is_even = pair % 2 == 0
    even_out[...] = jnp.where(is_even, after, before).astype(BF16)
    odd_out[...] = jnp.where(is_even, before, after).astype(BF16)
    own_ref[0:one] = segments[2]
    own_ref[one:rows] = segments[3]


def mix_kernel(
    pair_ref, small_ref, b_ref, even_ref, odd_ref, wq_ref, wo_ref, out_ref, query_part_ref, near_ref
):
    build_near(pair_ref, b_ref, even_ref, odd_ref, near_ref)
    rows, width = b_ref.shape
    one, half = rows // PAIR, width // 2
    reduce_mat = head_lanes(width)
    mixed = jnp.zeros((rows, width), F32)
    for i in range(len(ORDERED)):
        mixed = mixed + dot_t(small_ref[i], reduce_mat) * near_ref[i * one : i * one + rows]
    mixed = (mixed * lane_scale(mixed.shape)).astype(BF16)
    query_part_ref[...] = dot(mixed[:, :half], wq_ref[...])
    out_ref[...] = dot(mixed[:, half:], wo_ref[...]).astype(BF16)


def join_kernel(core_ref, both_ref, out_ref, sum_ref):
    sum_ref[...] = both_ref[0].astype(F32) + both_ref[1].astype(F32)
    second = core_ref[0] == 1
    share = out_ref.shape[0] // (PAIR * SHARDS)
    for part in range(PAIR * SHARDS):
        start = part * 2 * share
        out_ref[part * share : (part + 1) * share] = jnp.where(
            second, sum_ref[start + share : start + 2 * share], sum_ref[start : start + share]
        )


def back_kernel(out_ref, query_part_ref, own_ref, odd_ref, even_ref, wk_ref, wv_ref, parts_ref, rows_ref):
    width = own_ref.shape[1] // 2
    half = rows_ref.shape[0] // parts_ref.shape[0]
    share = half // 2
    total = own_ref[...] + even_ref[...].astype(F32) + odd_ref[...].astype(F32)
    total = total.astype(BF16)
    rows_ref[...] = (
        query_part_ref[...]
        + dot(total[:, :width], wk_ref[...])
        + dot(total[:, width:], wv_ref[...])
    )
    for part in range(PAIR * SHARDS):
        grads = rows_ref[part * half : (part + 1) * half]
        out = out_ref[part * share : (part + 1) * share]
        parts_ref[part] = jnp.concatenate(packed(grads) + packed(out), axis=0).astype(BF16)


def finish_kernel(x_ref, cot_ref, gain_ref, parts_ref, block_ref, grads_ref):
    rows = x_ref.shape[0]
    out, hidden_grads = [], []
    for h in range(PAIR):
        parts = [parts_ref[h * SHARDS + s].astype(F32) for s in range(SHARDS)]
        first, second = parts[0] + parts[2], parts[1] + parts[3]
        hidden_grads.append(unpacked(first[:rows] + second[:rows]))
        out += [unpacked(first[rows:]), unpacked(second[rows:])]
    out = jnp.concatenate(out, axis=0)
    hidden_grads = jnp.concatenate(hidden_grads, axis=0)
    x = x_ref[...].astype(F32)
    block_ref[...] = (x + out).astype(BF16)
    normed, inverse = normalized(x)
    scaled = hidden_grads * gain_ref[...].astype(F32).reshape(1, -1)
    layer_grads = inverse * (
        scaled
        - jnp.mean(scaled, axis=-1, keepdims=True)
        - normed * jnp.mean(scaled * normed, axis=-1, keepdims=True)
    )
    grads_ref[...] = (cot_ref[...].astype(F32) + layer_grads).astype(BF16)


def call(kernel, out_shape, in_specs, scratch=(), cost=0):
    return pl.pallas_call(
        kernel,
        out_shape=out_shape,
        in_specs=in_specs,
        out_specs=jax.tree.map(lambda _: VMEM, out_shape),
        scratch_shapes=list(scratch),
        compiler_params=PARAMS,
        cost_estimate=pl.CostEstimate(flops=cost, bytes_accessed=0, transcendentals=0),
    )


def exchanged(block, first):
    count = lax.axis_size("pair")
    route = []
    for i in range(first, count - 1, 2):
        route += [(i, i + 1), (i + 1, i)]
    return lax.ppermute(block, "pair", route)


def per_device(inputs, cotangent, norm_gain, query_weight, key_weight, value_weight, output_weight):
    pair = lax.axis_index("pair").astype(jnp.int32).reshape(1)
    frames = lax.axis_size("pair") * PAIR
    piece, channels = inputs.shape[2:]
    rows, local = piece * SHARDS, query_weight.shape[1]
    x = inputs.reshape(piece, channels)
    cot = cotangent.reshape(piece, channels)
    gain = norm_gain
    wq, wk, wv, wo = query_weight.T, key_weight.T, value_weight.T, output_weight
    shape = jax.ShapeDtypeStruct
    wide = shape((rows, 2 * local), BF16)
    row_scratch = pltpu.VMEM((rows, channels), F32)
    near_scratch = pltpu.VMEM((3 * rows, 2 * local), F32)

    packed_rows, packed_width = 2 * piece, channels // 2
    halves = [block.reshape(PAIR, piece // PAIR, channels) for block in (x, cot)]
    halves = jnp.concatenate(halves, axis=1)
    halves = lax.all_to_all(halves, "half", 0, 0)
    own_rows = shape((packed_rows, packed_width), BF16)
    hidden, cot_rows = call(norm_kernel, (own_rows, own_rows), [VMEM] * 2, cost=COST)(halves, gain)
    hidden = lax.all_gather(hidden, "space", axis=0)
    b = call(key_value_kernel, wide, [VMEM] * 3, [row_scratch])(hidden, wk, wv)
    near = [exchanged(b, first) for first in (0, 1)]
    cot_rows = lax.all_gather(cot_rows, "space", axis=0)
    a = call(query_kernel, wide, [VMEM] * 4, [row_scratch])(hidden, cot_rows, wq, wo)
    *sends, own, small = call(
        functools.partial(attend_kernel, frames),
        (wide, wide, shape((rows, 2 * local), F32), shape((len(ORDERED), rows, 256), BF16)),
        [SMEM] + [VMEM] * 4,
        [near_scratch],
    )(pair, a, b, *near)
    arrived = [exchanged(sends[first], first) for first in (1, 0)]
    out, query_part = call(
        mix_kernel,
        (shape((rows, channels), BF16), shape((rows, channels), F32)),
        [SMEM] + [VMEM] * 6,
        [near_scratch],
    )(pair, small, b, *near, wq, wo)
    cores = [[s, s + 1] for s in range(0, SHARDS, 2)]
    out = lax.all_gather(out, "space", axis=0, axis_index_groups=cores)
    core = (lax.axis_index("space") % 2).astype(jnp.int32).reshape(1)
    out = call(join_kernel, shape((rows // 2, channels), F32), [SMEM, VMEM], [row_scratch])(core, out)
    parts = call(
        back_kernel,
        shape((PAIR * SHARDS, packed_rows // PAIR + piece // 2, packed_width), BF16),
        [VMEM] * 7,
        [row_scratch],
    )(out, query_part, own, *arrived, wk, wv)
    parts = lax.all_to_all(parts, ("half", "space"), 0, 0)
    block, grads = call(
        finish_kernel, (shape((piece, channels), BF16), shape((piece, channels), BF16)), [VMEM] * 4
    )(x, cot, gain, parts)
    return block.reshape(inputs.shape), grads.reshape(inputs.shape)


def solution(mesh):
    devices = mesh.devices.reshape(-1, PAIR, SHARDS)
    mesh = Mesh(devices, ("pair", "half", "space"))
    frames = ("pair", "half")
    placed = (
        P(frames, None, "space", None),
        P(frames, None, "space", None),
        P(),
        P(None, "space"),
        P(None, "space"),
        P(None, "space"),
        P("space", None),
    )
    return jax.shard_map(
        per_device,
        mesh=mesh,
        in_specs=placed,
        out_specs=(P(frames, None, "space", None), P(frames, None, "space", None)),
        check_vma=False,
    )
```
